128 devices in a mesh: node: 16 (over z_lo, y, core), chip: 8 (over x, z_hi).
Axes of the slice: x: 4, y: 4, z: 4 (z_hi: 2, z_lo: 2; z = z_hi * 2 + z_lo), core: 2. Of those that a mesh axis runs over, the one named last changes fastest.
Arguments:
- tokens: bfloat16 [256, 256, 1152], P(('node', 'chip')), may hold values from -24 to 24
- cotangent: bfloat16 [256, 256, 1152], P(('node', 'chip')), may hold values from -24 to 24
- w_qkv_space: bfloat16 [1152, 1728], replicated, may hold values from -0.1875 to 0.1875
- w_out_space: bfloat16 [576, 1152], replicated, may hold values from -0.25 to 0.25
- w_qkv_time: bfloat16 [1152, 1728], replicated, may hold values from -0.1875 to 0.1875
- w_out_time: bfloat16 [576, 1152], replicated, may hold values from -0.25 to 0.25
Outputs:
- grad_tokens: bfloat16 [256, 256, 1152], P(('node', 'chip'))
- grad_qkv_space: float32 [1152, 1728], P(('node', 'chip'))
- grad_out_space: float32 [576, 1152], P(None, ('node', 'chip'))
- grad_qkv_time: float32 [1152, 1728], P(('node', 'chip'))
- grad_out_time: float32 [576, 1152], P(None, ('node', 'chip'))
The draws below stay inside these ranges and needn't reach their ends.
All inputs are finite; a program needn't handle non-finite values.
Results may differ from the reference program's by a relative error of at most 0.04.
The reference program's roundings to bfloat16 on the way count: a program that leaves them out, or rounds other values in their place, can miss the bound.
Values may be sent and summed in bfloat16 or wider, within the bound.
A program may use at most 192 MiB of HBM per device.

```python
import jax
import jax.numpy as jnp
from jax import lax

D = 1152
HEADS = 8
HEAD = 72
S = 256
INNER = 576
FRAMES = 256


def with_spikes(result, rng, source, target, blocks, factor):
    def block_of(axis_at):
        return (jnp.arange(result.shape[axis_at]) // (result.shape[axis_at] // blocks)).reshape((-1,) + (1,) * (result.ndim - 1 - axis_at))

    first = jax.random.permutation(rng, blocks)[block_of(target)]
    far = (block_of(target) + blocks // 2) % blocks
    return jnp.where((block_of(source) == first) | (block_of(source) == far), factor * result, result)


def block_scale(own_key, extent, split, low, largest):
    def one(axis_at, shards_of):
        steps = jax.random.uniform(jax.random.fold_in(jax.random.fold_in(own_key, 6), axis_at), (shards_of,), jnp.float32, low / len(split), largest / len(split))
        return jnp.repeat(jnp.exp(steps), extent[axis_at] // shards_of).reshape((-1,) + (1,) * (len(extent) - axis_at - 1))

    loudness = one(*split[0])
    for cut in split[1:]:
        loudness = loudness * one(*cut)
    return loudness


def normal_values(key, shape, spread, most, shards=(), kind=jnp.bfloat16):
    level = block_scale(key, shape, shards, -0.22, 0.18) if shards else 1.0
    values = jax.random.normal(key, shape, jnp.float32) * spread * level
    return jnp.minimum(jnp.maximum(values, -most), most).astype(kind)


def gaussian_with(key, shape, width, most, split, heavy, held_as=jnp.bfloat16):
    entries = width * jax.random.normal(key, shape, jnp.float32)
    if split:
        entries = entries * block_scale(key, shape, split, -0.22, 0.18)
    return jnp.clip(with_spikes(entries, jax.random.fold_in(key, 3), *heavy), -most, most).astype(held_as)


def setup_inputs(seed: int = 0) -> dict:
    splits = jax.random.split(jax.random.key(seed), 7)
    return {
        "tokens": gaussian_with(splits[0], (FRAMES, S, D), 1.0, 24.0, ((0, 128),), (0, 2, 128, 5.5)),
        "cotangent": gaussian_with(splits[1], (FRAMES, S, D), 1.0, 24.0, ((0, 128),), (0, 2, 128, 5.5)),
        "w_qkv_space": normal_values(splits[2], (D, 3 * INNER), D ** -0.5, 0.1875),
        "w_out_space": normal_values(splits[3], (INNER, D), INNER ** -0.5, 0.25),
        "w_qkv_time": normal_values(splits[4], (D, 3 * INNER), D ** -0.5, 0.1875),
        "w_out_time": normal_values(splits[5], (INNER, D), INNER ** -0.5, 0.25),
    }


def seq_forward(query_part, key_part, value_part):
    score_scale = HEAD ** -0.5
    scores = jnp.einsum("lhe,mhe->hlm", query_part.astype(jnp.float32), key_part.astype(jnp.float32)) * score_scale
    exp_scores = jnp.exp(scores)
    attn_prob = exp_scores / jnp.sum(exp_scores, axis=-1, keepdims=True)
    prob_low = attn_prob.astype(jnp.bfloat16)
    attended = jnp.einsum("hlm,mhe->lhe", prob_low.astype(jnp.float32), value_part.astype(jnp.float32)).astype(jnp.bfloat16)
    return attn_prob, prob_low, attended


def seq_backward(query_part, key_part, value_part, grad_attn):
    score_scale = HEAD ** -0.5
    attn_prob, prob_low, attended = seq_forward(query_part, key_part, value_part)
    grad_value = jnp.einsum("hlm,lhe->mhe", prob_low.astype(jnp.float32), grad_attn.astype(jnp.float32)).astype(jnp.bfloat16)
    grad_prob = jnp.einsum("lhe,mhe->hlm", grad_attn.astype(jnp.float32), value_part.astype(jnp.float32))
    centred = grad_prob - jnp.sum(attn_prob * grad_prob, axis=-1, keepdims=True)
    grad_score = (attn_prob * centred * score_scale).astype(jnp.bfloat16)
    grad_query = jnp.einsum("hlm,mhe->lhe", grad_score.astype(jnp.float32), key_part.astype(jnp.float32)).astype(jnp.bfloat16)
    grad_key = jnp.einsum("hlm,lhe->mhe", grad_score.astype(jnp.float32), query_part.astype(jnp.float32)).astype(jnp.bfloat16)
    return jnp.stack([grad_query, grad_key, grad_value], axis=1)


def project(hidden, weight):
    rows = hidden.reshape(-1, D)
    joined = jnp.dot(rows, weight, preferred_element_type=jnp.float32).astype(jnp.bfloat16)
    return joined.reshape(hidden.shape[0], hidden.shape[1], 3, HEADS, HEAD)


def attend(qkv_all):
    def single(items):
        return seq_forward(items[0], items[1], items[2])[2]
    return lax.map(single, (qkv_all[:, :, 0], qkv_all[:, :, 1], qkv_all[:, :, 2]))


def block_output(hidden, attended, weight_out):
    summed = hidden.reshape(-1, D).astype(jnp.float32) + jnp.dot(attended.reshape(-1, INNER), weight_out, preferred_element_type=jnp.float32)
    return summed.astype(jnp.bfloat16).reshape(hidden.shape)


def backward(hidden, qkv_all, attended, upstream, weight_qkv, weight_out):
    up_rows = upstream.reshape(-1, D)
    grad_attn = jnp.dot(up_rows, weight_out.T, preferred_element_type=jnp.float32).astype(jnp.bfloat16).reshape(attended.shape)
    grad_out = jnp.dot(attended.reshape(-1, INNER).T, up_rows, preferred_element_type=jnp.float32)

    def single(items):
        return seq_backward(items[0], items[1], items[2], items[3])

    grad_act = lax.map(single, (qkv_all[:, :, 0], qkv_all[:, :, 1], qkv_all[:, :, 2], grad_attn))
    grad_rows = grad_act.reshape(-1, 3 * INNER)
    grad_qkv = jnp.dot(hidden.reshape(-1, D).T, grad_rows, preferred_element_type=jnp.float32)
    grad_input = up_rows.astype(jnp.float32) + jnp.dot(grad_rows, weight_qkv.T, preferred_element_type=jnp.float32)
    return grad_input.astype(jnp.bfloat16).reshape(hidden.shape), grad_qkv, grad_out


def reference(tokens, cotangent, w_qkv_space, w_out_space, w_qkv_time, w_out_time):
    qkv_space = project(tokens, w_qkv_space)
    attended_space = attend(qkv_space)
    hidden_mid = block_output(tokens, attended_space, w_out_space)
    mid_time = jnp.swapaxes(hidden_mid, 0, 1)
    upstream_time = jnp.swapaxes(cotangent, 0, 1)
    qkv_time = project(mid_time, w_qkv_time)
    attended_time = attend(qkv_time)
    grad_mid_time, grad_qkv_time, grad_out_time = backward(mid_time, qkv_time, attended_time, upstream_time, w_qkv_time, w_out_time)
    grad_mid = jnp.swapaxes(grad_mid_time, 0, 1)
    grad_tokens, grad_qkv_space, grad_out_space = backward(tokens, qkv_space, attended_space, grad_mid, w_qkv_space, w_out_space)
    return grad_tokens, grad_qkv_space, grad_out_space, grad_qkv_time, grad_out_time
```

```python
import jax
import jax.numpy as jnp
from jax import lax
from jax.experimental import pallas as pl
from jax.experimental.pallas import tpu as pltpu
from jax.sharding import PartitionSpec as P

D = 1152
HEADS = 8
HEAD = 72
INNER = 576
S = 256
N = 128
LANES = 384
F32 = jnp.float32
BF = jnp.bfloat16
MESH = pl.DeviceIdType.MESH
SCALE = HEAD ** (-0.5)


def place(d):
    return {"node": d // 8, "chip": lax.rem(d, 8)}


def mm(a, b):
    return jnp.dot(a, b, preferred_element_type=F32)


def mm_nt(a, b):
    return lax.dot_general(a, b, (((1,), (1,)), ((), ())), preferred_element_type=F32)


def mm_tn(a, b):
    return lax.dot_general(a, b, (((0,), (0,)), ((), ())), preferred_element_type=F32)


def probabilities(q, k):
    e = jnp.exp(mm_nt(q, k) * SCALE)
    return e * (1.0 / jnp.sum(e, axis=-1, keepdims=True))


def head_columns(part, h):
    return pl.ds(part * INNER + h * HEAD, HEAD)


def head_backward(p, low, q, k, v, ga):
    gv = mm_tn(low, ga).astype(BF)
    gp = mm_nt(ga, v)
    centred = gp - jnp.sum(p * gp, axis=-1, keepdims=True)
    gs = (p * centred * SCALE).astype(BF)
    return mm(gs, k).astype(BF), mm_tn(gs, q).astype(BF), gv


def rotate(b, s):
    s %= 6
    return ((b << s) | (b >> (6 - s))) & 63


class Reduce:
    def __init__(self, where, acc, acc_odd, out, out_odd, first, first_odd, later, later_odd,
                 fin, fin_odd, got, got_odd, ssem, rsem, fsem):
        self.where = where
        self.acc, self.acc_odd = acc, acc_odd
        self.out, self.out_odd = out, out_odd
        self.first, self.first_odd = first, first_odd
        self.later, self.later_odd = later, later_odd
        self.fin, self.fin_odd, self.got, self.got_odd = fin, fin_odd, got, got_odd
        self.ssem, self.rsem, self.fsem = ssem, rsem, fsem
        self.base = [0, 0, 0]
        self.sent = []

    def copy(self, src, dst, a, step, which, target):
        return pltpu.make_async_remote_copy(
            src_ref=src, dst_ref=dst, send_sem=self.ssem.at[a, step, which], recv_sem=self.rsem.at[a, step, which],
            device_id=target, device_id_type=MESH)

    def core_copies(self, a):
        target = self.where["mate"]
        return (self.copy(self.out.at[a], self.first.at[a], a, 0, 0, target),
                self.copy(self.out_odd.at[a], self.first_odd.at[a], a, 0, 1, target))

    @staticmethod
    def put(value, main, odd, a, turn):
        rows = value[0:1024].reshape(64, 16, LANES).astype(BF)
        rest = value[1024:1152].reshape(64, 2, LANES).astype(BF)
        for b in range(64):
            main[a, rotate(b, turn)] = rows[b]
            odd[a, rotate(b, turn)] = rest[b]

    def start(self, product):
        core = self.where["core"]
        for mine in (0, 1):
            @pl.when(core == mine)
            def _():
                for a in (2, 1, 0):
                    self.put(product(3 * (1 - mine) + a), self.out, self.out_odd, a, 2 * a + 1 - mine)
                    for c in self.core_copies(a):
                        c.start()
                for a in (2, 1, 0):
                    self.put(product(3 * mine + a), self.acc, self.acc_odd, a, 2 * a + mine)

    def step_copies(self, a, t):
        core, bits, mates = self.where["core"], self.where["bits"], self.where["mates"]
        half = 32 >> t
        i, j = (2 * a + t) % 6, (2 * a + 1 + t) % 6
        bit = bits[i] * (1 - core) + bits[j] * core
        mate = mates[i] * (1 - core) + mates[j] * core
        away = self.base[a] + (1 - bit) * half
        keep = self.base[a] + bit * half
        target = place(mate)
        spot = pl.ds(64 - 2 * half, half)
        return keep, half, (
            self.copy(self.acc.at[a, pl.ds(away, half)], self.later.at[a, spot], a, t + 1, 0, target),
            self.copy(self.acc_odd.at[a, pl.ds(away, half)], self.later_odd.at[a, spot], a, t + 1, 1, target))

    def send_step(self, a, t):
        keep, half, copies = self.step_copies(a, t)
        for c in copies:
            c.start()
        self.sent.append(copies)
        self.base[a] = keep
        return copies

    def begin(self):
        self.flying = [None] * 3
        for a in (2, 1, 0):
            for c in self.core_copies(a):
                c.wait_recv()
            self.acc[a] = self.acc[a] + self.first[a]
            self.acc_odd[a] = self.acc_odd[a] + self.first_odd[a]
            self.flying[a] = self.send_step(a, 0)

    def step(self, t):
        half = 32 >> t
        for a in (2, 1, 0):
            for c in self.flying[a]:
                c.wait_recv()
            base, spot = self.base[a], 64 - 2 * half
            if t < 5:
                self.acc[a, pl.ds(base, half)] = self.acc[a, pl.ds(base, half)] + self.later[a, pl.ds(spot, half)]
                self.acc_odd[a, pl.ds(base, half)] = (
                    self.acc_odd[a, pl.ds(base, half)] + self.later_odd[a, pl.ds(spot, half)])
                self.flying[a] = self.send_step(a, t + 1)
            else:
                total = self.acc[a, base].astype(F32) + self.later[a, spot].astype(F32)
                rest = self.acc_odd[a, base].astype(F32) + self.later_odd[a, spot].astype(F32)
                lanes = pl.ds(a * LANES, LANES)
                self.fin[0, :, lanes] = total[0:8]
                self.fin[1, :, lanes] = total[8:16]
                self.fin_odd[0, :, lanes] = rest[0:1]
                self.fin_odd[1, :, lanes] = rest[1:2]

    def final_copies(self):
        core = self.where["core"]
        pairs = ((self.fin, self.got), (self.fin_odd, self.got_odd))
        return [pltpu.make_async_remote_copy(
            src_ref=src.at[1 - core], dst_ref=dst, send_sem=self.fsem.at[0, i], recv_sem=self.fsem.at[1, i],
            device_id=self.where["mate"], device_id_type=MESH) for i, (src, dst) in enumerate(pairs)]

    def finish(self, out_qkv, out_out):
        core = self.where["core"]
        copies = self.final_copies()
        for c in copies:
            c.start()
        for c in copies:
            c.wait_recv()
        for mine in (0, 1):
            @pl.when(core == mine)
            def _():
                for own, got, rows in ((self.fin, self.got, pl.ds(0, 8)), (self.fin_odd, self.got_odd, pl.ds(8, 1))):
                    left, right = (own[0], got[...]) if mine == 0 else (got[...], own[1])
                    out_qkv[rows, 0:D] = left
                    out_qkv[rows, D:1728] = right[:, 0:INNER]
                    out_out[rows, :] = right[:, INNER:D]

    def drain(self):
        for a in range(3):
            for c in self.core_copies(a):
                c.wait_send()
        for copies in self.sent:
            for c in copies:
                c.wait_send()
        for c in self.final_copies():
            c.wait_send()


def kernel(tokens, cotangent, w_qkv_space, w_out_space, w_qkv_time, w_out_time,
           grad_tokens, gq_space, go_space, gq_time, go_time,
           tok, cot, wqs, wos, wqt, wot,
           snd_c, rcv_c, snd_m, rcv_m, snd_r, rcv_r,
           qkv_s, qkv_t, ga_ref, act, attp_t, attp_s, h_t, g_t, perm, weave, part,
           out_m, out_o, acc_tm, acc_to, first_tm, first_to, later_tm, later_to,
           acc_sm, acc_so, first_sm, first_so, later_sm, later_so,
           fin_t, fin_to, got_t, got_to, fin_s, fin_so, got_s, got_so,
           load_sem, local_sem, a2a_send, a2a_recv, rs_send_t, rs_recv_t, fin_sem_t, rs_send_s, rs_recv_s, fin_sem_s):
    node, chip = lax.axis_index("node"), lax.axis_index("chip")
    me = node * 8 + chip
    barrier = pltpu.get_barrier_semaphore()

    def others(body):
        @pl.loop(0, 18)
        def _(i):
            for u in range(7):
                body(lax.rem(me + 1 + i * 7 + u, N))
        body(lax.rem(me + 127, N))

    others(lambda d: pl.semaphore_signal(barrier, inc=1, device_id=place(d), device_id_type=MESH))

    loads = [pltpu.make_async_copy(src, dst, load_sem.at[i]) for i, (src, dst) in enumerate(
        ((cotangent, cot), (tokens, tok), (w_qkv_space, wqs), (w_out_space, wos), (w_qkv_time, wqt), (w_out_time, wot)))]
    for c in loads:
        c.start()

    core = lax.rem(node, 2)
    x, y, z = chip // 2, lax.rem(node // 2, 4), lax.rem(chip, 2) * 2 + node // 8

    def index(x, y, z, core):
        return lax.rem(z, 2) * 64 + y * 16 + core * 8 + x * 2 + z // 2

    def coded(i):
        return i // 2, lax.rem(i // 2 + i, 2), 3 - i, i + 1 - 2 * lax.rem(i, 2)

    xu, xv, x_far, x_near = coded(x)
    yu, yv, y_far, y_near = coded(y)
    zu, zv, z_far, z_near = coded(z)
    where = {
        "core": core, "mate": place(index(x, y, z, 1 - core)), "bits": (xu, xv, yu, yv, zu, zv),
        "mates": (index(x_far, y, z, core), index(x_near, y, z, core), index(x, y_far, z, core),
                  index(x, y_near, z, core), index(x, y, z_far, core), index(x, y, z_near, core)),
    }

    to = lax.broadcasted_iota(jnp.int32, (S, S), 0)
    fro = lax.broadcasted_iota(jnp.int32, (S, S), 1)
    weave[...] = jnp.where((to % 2) * 128 + to // 2 == fro, 1.0, 0.0).astype(BF)

    def pieces(rows_of, c, dst):
        both = jnp.concatenate([rows_of[0, pl.ds(c * 128, 128)], rows_of[1, pl.ds(c * 128, 128)]], axis=0)
        dst[c] = mm(weave[...], both).astype(BF).reshape(128, 2, D)

    def exchange(kind, c, src, dst):
        pltpu.make_async_copy(src.at[c, me], dst.at[c, me], local_sem.at[kind, c]).start()
        others(lambda d: pltpu.make_async_remote_copy(
            src_ref=src.at[c, d], dst_ref=dst.at[c, me], send_sem=a2a_send.at[kind, c], recv_sem=a2a_recv.at[kind, c],
            device_id=place(d), device_id_type=MESH).start())

    def whole(kind, c, src, dst):
        return pltpu.make_async_remote_copy(
            src_ref=src.at[c, pl.ds(0, N - 1)], dst_ref=dst.at[c, pl.ds(0, N - 1)], send_sem=a2a_send.at[kind, c],
            recv_sem=a2a_recv.at[kind, c], device_id=where["mate"], device_id_type=MESH)

    def arrived(kind, c, src, dst):
        whole(kind, c, src, dst).wait_recv()
        pltpu.make_async_copy(src.at[c, me], dst.at[c, me], local_sem.at[kind, c]).wait()

    loads[0].wait()
    for c in (0, 1):
        pieces(cot, c, snd_c)

    def sources(code, pair, row):
        def plain(two):
            return (two // 2) * 2 + (two // 2 + two) % 2
        gx, gy, gz = plain(code // 16), plain((code // 4) % 4), plain(code % 4)
        return 9 * ((gz % 2) * 64 + gy * 16 + pair * 8 + gx * 2 + gz // 2) + row

    at = lax.broadcasted_iota(jnp.int32, (1024, 1), 0)
    perm[0:1024, :] = jnp.where(
        sources(at // 16, (at // 8) % 2, at % 8) == lax.broadcasted_iota(jnp.int32, (1024, D), 1), 1.0, 0.0).astype(BF)
    at = lax.broadcasted_iota(jnp.int32, (128, 1), 0)
    perm[1024:D, :] = jnp.where(
        sources(at // 2, at % 2, 8) == lax.broadcasted_iota(jnp.int32, (128, D), 1), 1.0, 0.0).astype(BF)
    act[:, 1728:1920] = jnp.zeros((512, 192), BF)
    attp_t[:, 0:192] = jnp.zeros((512, 192), BF)
    attp_s[:, 0:192] = jnp.zeros((512, 192), BF)

    pl.semaphore_wait(barrier, N - 1)
    for c in (0, 1):
        exchange(0, c, snd_c, rcv_c)

    loads[1].wait()
    loads[2].wait()
    loads[3].wait()

    @pl.loop(0, 2)
    def _(f):
        rows = pl.ds(pl.multiple_of(f * S, S), S)
        hidden = tok[f]
        qkv_s[f] = mm(hidden, wqs[...]).astype(BF)
        for h in range(HEADS):
            q, k, v = (qkv_s[f, :, head_columns(i, h)] for i in range(3))
            low = probabilities(q, k).astype(BF)
            attp_s[rows, pl.ds(192 + HEAD * h, HEAD)] = mm(low, v).astype(BF)
        cot[f] = (hidden.astype(F32) + mm(attp_s[rows, 192:768], wos[...])).astype(BF)

    for c in (0, 1):
        pieces(cot, c, snd_m)
        exchange(1, c, snd_m, rcv_m)

    loads[4].wait()
    loads[5].wait()

    @pl.loop(0, 2)
    def _(c):
        rows = pl.ds(pl.multiple_of(c * S, S), S)
        arrived(0, c, snd_c, rcv_c)
        ga_ref[...] = mm_nt(rcv_c[c].reshape(S, D), wot[...]).astype(BF)
        arrived(1, c, snd_m, rcv_m)
        qkv_t[...] = mm(rcv_m[c].reshape(S, D), wqt[...]).astype(BF)
        for h in range(HEADS):
            q, k, v = (qkv_t[:, head_columns(i, h)] for i in range(3))
            ga = ga_ref[:, head_columns(0, h)]
            p = probabilities(q, k)
            low = p.astype(BF)
            attp_t[rows, pl.ds(192 + HEAD * h, HEAD)] = mm(low, v).astype(BF)
            grads = head_backward(p, low, q, k, v, ga)
            for i in range(3):
                act[rows, head_columns(i, h)] = grads[i]
        up = rcv_c[c].reshape(S, D)
        back = (up.astype(F32) + mm_nt(act[rows, 0:1728], wqt[...])).astype(BF)
        snd_r[c] = back.reshape(128, 2, D)
        exchange(2, c, snd_r, rcv_r)
        h_t[:, rows] = mm_nt(perm[...], rcv_m[c].reshape(S, D)).astype(BF)
        g_t[:, rows] = mm_nt(perm[...], rcv_c[c].reshape(S, D)).astype(BF)

    def product_of(attp):
        def product(chunk):
            lanes = pl.ds(chunk * LANES, LANES)
            if chunk < 4:
                return mm(h_t[...], act[:, lanes])
            right = mm(g_t[...], attp[:, pl.ds((chunk - 4) * LANES, LANES)])
            return right + mm(h_t[...], act[:, lanes]) if chunk == 4 else right
        return product

    time = Reduce(where, acc_tm, acc_to, out_m.at[0], out_o.at[0], first_tm, first_to, later_tm, later_to,
                  fin_t, fin_to, got_t, got_to, rs_send_t, rs_recv_t, fin_sem_t)
    space = Reduce(where, acc_sm, acc_so, out_m.at[1], out_o.at[1], first_sm, first_so, later_sm, later_so,
                   fin_s, fin_so, got_s, got_so, rs_send_s, rs_recv_s, fin_sem_s)
    time.start(product_of(attp_t))
    time.begin()

    for f in (0, 1):
        h_t[:, f * S:(f + 1) * S] = mm_nt(perm[...], tok[f]).astype(BF)
    for c in (0, 1):
        arrived(2, c, snd_r, rcv_r)
        both = mm_tn(weave[...], rcv_r[c].reshape(S, D)).astype(BF)
        cot[0, pl.ds(c * 128, 128)] = both[0:128]
        cot[1, pl.ds(c * 128, 128)] = both[128:256]
    time.step(0)

    for f in (0, 1):
        rows = pl.ds(f * S, S)
        up = cot[f]
        ga_ref[...] = mm_nt(up, wos[...]).astype(BF)
        g_t[:, rows] = mm_nt(perm[...], up).astype(BF)
        for h in range(HEADS):
            q, k, v = (qkv_s[f, :, head_columns(i, h)] for i in range(3))
            p = probabilities(q, k)
            grads = head_backward(p, p.astype(BF), q, k, v, ga_ref[:, head_columns(0, h)])
            for i in range(3):
                act[rows, head_columns(i, h)] = grads[i]
            if h == 3:
                time.step(1 + 2 * f)
        time.step(2 + 2 * f)
    space.start(product_of(attp_s))
    time.step(5)
    space.begin()
    for f in (0, 1):
        rows = pl.ds(f * S, S)
        grad_tokens[f] = (cot[f].astype(F32) + mm_nt(act[rows, 0:1728], wqs[...])).astype(BF)
    time.finish(gq_time, go_time)
    for t in range(6):
        space.step(t)
    space.finish(gq_space, go_space)

    for kind, (src, dst) in enumerate(((snd_c, rcv_c), (snd_m, rcv_m), (snd_r, rcv_r))):
        for c in (0, 1):
            whole(kind, c, src, dst).wait_send()
    time.drain()
    space.drain()


def body(tokens, cotangent, w_qkv_space, w_out_space, w_qkv_time, w_out_time):
    vm = pltpu.VMEM
    pieces = vm((2, N, 2, D), BF)

    def main(n):
        return vm((3, n, 16, LANES), BF)

    def odd(n):
        return vm((3, n, 2, LANES), BF)

    def ends():
        return [vm((2, 8, D), F32), vm((2, 1, D), F32), vm((8, D), F32), vm((1, D), F32)]

    dma = pltpu.SemaphoreType.DMA
    halves = [main(64), odd(64), main(64), odd(64), main(63), odd(63)]
    sums = [dma((3, 7, 2)), dma((3, 7, 2)), dma((2, 2))]
    hbm, inside = pl.BlockSpec(memory_space=pl.ANY), pl.BlockSpec(memory_space=pltpu.VMEM)
    grad_tokens, gq_space, go_space, gq_time, go_time = pl.pallas_call(
        kernel,
        out_shape=(
            jax.ShapeDtypeStruct((2, S, D), BF),
            jax.ShapeDtypeStruct((9, 1728), F32),
            jax.ShapeDtypeStruct((9, INNER), F32),
            jax.ShapeDtypeStruct((9, 1728), F32),
            jax.ShapeDtypeStruct((9, INNER), F32),
        ),
        in_specs=[hbm] * 6,
        out_specs=(inside,) * 5,
        scratch_shapes=[
            vm((2, S, D), BF), vm((2, S, D), BF), vm((D, 1728), BF), vm((INNER, D), BF), vm((D, 1728), BF), vm((INNER, D), BF),
            *[pieces] * 6,
            vm((2, S, 1728), BF), vm((S, 1728), BF), vm((S, INNER), BF), vm((512, 1920), BF), vm((512, 768), BF), vm((512, 768), BF),
            vm((D, 512), BF), vm((D, 512), BF), vm((D, D), BF), vm((S, S), BF), vm((8, 128), F32),
            vm((2, 3, 64, 16, LANES), BF), vm((2, 3, 64, 2, LANES), BF),
            *halves, *halves, *ends(), *ends(),
            dma((6,)), dma((3, 2)), dma((3, 2)), dma((3, 2)), *sums, *sums,
        ],
        compiler_params=pltpu.CompilerParams(
            collective_id=0, has_side_effects=True, vmem_limit_bytes=63 * 2**20),
    )(tokens, cotangent, w_qkv_space, w_out_space, w_qkv_time, w_out_time)
    return grad_tokens, gq_space, go_space.T, gq_time, go_time.T


def solution(mesh):
    rows = P(("node", "chip"), None, None)
    return jax.shard_map(
        body,
        mesh=mesh,
        in_specs=(rows, rows, P(), P(), P(), P()),
        out_specs=(rows, P(("node", "chip"), None), P(None, ("node", "chip")),
                   P(("node", "chip"), None), P(None, ("node", "chip"))),
        check_vma=False,
    )
```

```python
import jax
import jax.numpy as jnp
from jax import lax
from jax.experimental import pallas as pl
from jax.experimental.pallas import tpu as pltpu
from jax.sharding import PartitionSpec as P

D = 1152
HEADS = 8
HEAD = 72
INNER = 576
S = 256
N = 128
LANES = 384
F32 = jnp.float32
BF = jnp.bfloat16
MESH = pl.DeviceIdType.MESH
SCALE = HEAD ** (-0.5)
LOG2E = 1.4426950408889634


def place(d):
    return {"node": d // 8, "chip": lax.rem(d, 8)}


def device(x, y, z, core):
    return lax.rem(z, 2) * 64 + y * 16 + core * 8 + x * 2 + z // 2


def mm(a, b):
    return jnp.dot(a, b, preferred_element_type=F32)


def mm_nt(a, b):
    return lax.dot_general(a, b, (((1,), (1,)), ((), ())), preferred_element_type=F32)


def mm_tn(a, b):
    return lax.dot_general(a, b, (((0,), (0,)), ((), ())), preferred_element_type=F32)


def probabilities(q, k):
    e = jnp.exp2(mm_tn(k, q) * (SCALE * LOG2E))
    return e * (1.0 / jnp.sum(e, axis=0, keepdims=True))


def put_pair(ref, row, lanes, two):
    ref[pl.ds(row, 2 * HEAD), lanes] = jnp.concatenate(two, axis=0).astype(BF)


def heads(qkv, ga, act, att, lanes):
    for pair in range(HEADS // 2):
        found = [[], [], [], []]
        for h in (2 * pair, 2 * pair + 1):
            q, k, v = (qkv[pl.ds(i * INNER + h * HEAD, HEAD), :] for i in range(3))
            p = probabilities(q, k)
            low = p.astype(BF)
            if att is not None:
                found[3].append(mm(v, low))
            if act is not None:
                g = ga[pl.ds(h * HEAD, HEAD), :]
                gp = mm_tn(v, g)
                found[2].append(mm_nt(g, low))
                centred = gp - jnp.sum(p * gp, axis=0, keepdims=True)
                gs = (p * centred * SCALE).astype(BF)
                found[0].append(mm(k, gs))
                found[1].append(mm_nt(q, gs))
        if att is not None:
            put_pair(att, 192 + 2 * HEAD * pair, lanes, found[3])
        if act is not None:
            for i in range(3):
                put_pair(act, INNER * i + 2 * HEAD * pair, lanes, found[i])


def turned(b, a):
    return ((b << (2 * a)) | (b >> (6 - 2 * a))) & 63


class Reduce:
    def __init__(self, where, acc, acc_odd, out, out_odd, first, first_odd, near, near_odd, mid, mid_odd, far, far_odd,
                 ssem, rsem, fsem):
        self.where, self.core, self.at = where, where["core"], where["at"]
        self.acc, self.out, self.first = (acc, acc_odd), (out, out_odd), (first, first_odd)
        self.near, self.mid, self.far = (near, near_odd), (mid, mid_odd), (far, far_odd)
        self.ssem, self.rsem, self.fsem = ssem, rsem, fsem

    def copy(self, src, dst, a, step, which, target):
        return pltpu.make_async_remote_copy(
            src_ref=src, dst_ref=dst, send_sem=self.ssem.at[a, step, which], recv_sem=self.rsem.at[a, step, which],
            device_id=target, device_id_type=MESH)

    def core_copies(self, a):
        return [self.copy(self.out[w].at[a], self.first[w].at[a], a, 0, w, self.where["mate"]) for w in (0, 1)]

    def axis_copies(self, a):
        copies = []
        for step in (1, 2, 3):
            to = list(self.at)
            to[a] = lax.rem(to[a] + step, 4)
            block = pl.ds(to[a] * 16, 16)
            copies += [self.copy(self.acc[w].at[a, block], self.near[w].at[a, step - 1], a, step, w,
                                 place(device(*to, self.core))) for w in (0, 1)]
        return copies

    def plane(self, a):
        return self.at[(a + 1) % 3] * 4 + self.at[(a + 2) % 3]

    def plane_copies(self, a, o, k):
        to = list(self.at)
        to[(a + 1) % 3], to[(a + 2) % 3] = o // 4, lax.rem(o, 4)
        slot = self.core * 16 + self.plane(a)
        return [pltpu.make_async_remote_copy(
            src_ref=src, dst_ref=self.far[w].at[a, slot], send_sem=self.fsem.at[0, a, w], recv_sem=self.fsem.at[1, a, w],
            device_id=place(device(*to, k)), device_id_type=MESH)
            for w, src in ((0, self.mid[0].at[a, o, k]), (1, self.mid[1].at[a, o]))]

    def plane_whole(self, a, w):
        part = self.far[w].at[a, pl.ds(0, 31)]
        return pltpu.make_async_remote_copy(
            src_ref=part, dst_ref=part, send_sem=self.fsem.at[0, a, w], recv_sem=self.fsem.at[1, a, w],
            device_id=self.where["mate"], device_id_type=MESH)

    @staticmethod
    def put(value, main, odd, a):
        rows = value[0:1024].reshape(64, 16, LANES).astype(BF)
        rest = value[1024:1152].reshape(64, 2, LANES).astype(BF)
        for b in range(64):
            main[a, turned(b, a)] = rows[b]
            odd[a, turned(b, a)] = rest[b]

    def start(self, product):
        for mine in (0, 1):
            @pl.when(self.core == mine)
            def _():
                for a in (2, 1, 0):
                    self.put(product(3 * (1 - mine) + a), *self.out, a)
                    for c in self.core_copies(a):
                        c.start()
                for a in (2, 1, 0):
                    self.put(product(3 * mine + a), *self.acc, a)

    def begin(self):
        for a in (2, 1, 0):
            for c in self.core_copies(a):
                c.wait_recv()
            for w in (0, 1):
                self.acc[w][a] = self.acc[w][a] + self.first[w][a]
            for c in self.axis_copies(a):
                c.start()

    def spread(self):
        for a in (2, 1, 0):
            for c in self.axis_copies(a):
                c.wait_recv()
            mine = pl.ds(self.at[a] * 16, 16)
            total, rest = (self.acc[w][a, mine].astype(F32) + self.near[w][a, 0].astype(F32)
                           + self.near[w][a, 1].astype(F32) + self.near[w][a, 2].astype(F32) for w in (0, 1))
            self.mid[0][a] = total.reshape(16, 2, 8, LANES).astype(BF)
            self.mid[1][a] = rest.astype(BF)
            here = self.plane(a)
            for c in self.plane_copies(a, here, 1 - self.core):
                c.start()

            @pl.loop(1, 16)
            def _(step):
                o = lax.rem(here + step, 16)
                for k in (0, 1):
                    for c in self.plane_copies(a, o, k):
                        c.start()

    def finish(self, out_qkv, out_out):
        for a in (2, 1, 0):
            for w in (0, 1):
                self.plane_whole(a, w).wait_recv()
            here = self.plane(a)
            self.far[0][a, self.core * 16 + here] = self.mid[0][a, here, self.core]
            self.far[1][a, self.core * 16 + here] = self.mid[1][a, here]
            for half in (0, 1):
                chunk = 3 * half + a
                blocks = pl.ds(half * 16, 16)
                total = jnp.sum(self.far[0][a, blocks].astype(F32), axis=0)
                both = jnp.sum(self.far[1][a, blocks].astype(F32), axis=0)
                for rows, value in ((pl.ds(0, 8), total), (pl.ds(8, 1), jnp.where(self.core == 0, both[0:1], both[1:2]))):
                    if chunk < 4:
                        out_qkv[rows, chunk * LANES:(chunk + 1) * LANES] = value
                    elif chunk == 4:
                        out_qkv[rows, 1536:1728] = value[:, 0:192]
                        out_out[rows, 0:192] = value[:, 192:384]
                    else:
                        out_out[rows, 192:576] = value

    def drain(self):
        for a in range(3):
            for c in self.core_copies(a) + self.axis_copies(a):
                c.wait_send()
            for w in (0, 1):
                self.plane_whole(a, w).wait_send()


def kernel(tokens, cotangent, w_qkv_space, w_out_space, w_qkv_time, w_out_time,
           grad_tokens, gq_space, go_space, gq_time, go_time,
           tok, cot, wqs, wos, wqt, wot,
           snd_c, rcv_c, snd_m, rcv_m, snd_r, rcv_r,
           qkv_s, qkv_t, ga_ref, act, attp_t, attp_s, h_t, g_t, h_s, perm, weave, out_m, out_o, *rest):
    time_refs, space_refs = rest[0:10], rest[10:20]
    load_sem, local_sem, a2a_send, a2a_recv = rest[20:24]
    time_sems, space_sems = rest[24:27], rest[27:30]
    node, chip = lax.axis_index("node"), lax.axis_index("chip")
    me = node * 8 + chip
    barrier = pltpu.get_barrier_semaphore()

    def others(body):
        @pl.loop(0, 18)
        def _(i):
            for u in range(7):
                body(lax.rem(me + 1 + i * 7 + u, N))
        body(lax.rem(me + 127, N))

    others(lambda d: pl.semaphore_signal(barrier, inc=1, device_id=place(d), device_id_type=MESH))

    loads = [pltpu.make_async_copy(src, dst, load_sem.at[i]) for i, (src, dst) in enumerate(
        ((cotangent, cot), (tokens, tok), (w_qkv_space, wqs), (w_out_space, wos), (w_qkv_time, wqt), (w_out_time, wot)))]
    for c in loads:
        c.start()

    core = lax.rem(node, 2)
    x, y, z = chip // 2, lax.rem(node // 2, 4), lax.rem(chip, 2) * 2 + node // 8

    where = {"core": core, "at": (x, y, z), "mate": place(device(x, y, z, 1 - core))}

    to = lax.broadcasted_iota(jnp.int32, (S, S), 0)
    fro = lax.broadcasted_iota(jnp.int32, (S, S), 1)
    weave[...] = jnp.where((to % 2) * 128 + to // 2 == fro, 1.0, 0.0).astype(BF)

    def pieces(rows_of, c, dst):
        both = jnp.concatenate([rows_of[0, pl.ds(c * 128, 128)], rows_of[1, pl.ds(c * 128, 128)]], axis=0)
        dst[c] = mm(weave[...], both).astype(BF).reshape(128, 2, D)

    def exchange(kind, c, src, dst):
        pltpu.make_async_copy(src.at[c, me], dst.at[c, me], local_sem.at[kind, c]).start()
        others(lambda d: pltpu.make_async_remote_copy(
            src_ref=src.at[c, d], dst_ref=dst.at[c, me], send_sem=a2a_send.at[kind, c], recv_sem=a2a_recv.at[kind, c],
            device_id=place(d), device_id_type=MESH).start())

    def whole(kind, c, src, dst):
        return pltpu.make_async_remote_copy(
            src_ref=src.at[c, pl.ds(0, N - 1)], dst_ref=dst.at[c, pl.ds(0, N - 1)], send_sem=a2a_send.at[kind, c],
            recv_sem=a2a_recv.at[kind, c], device_id=where["mate"], device_id_type=MESH)

    def arrived(kind, c, src, dst):
        whole(kind, c, src, dst).wait_recv()
        pltpu.make_async_copy(src.at[c, me], dst.at[c, me], local_sem.at[kind, c]).wait()

    with jax.named_scope("load_cotangent"):
        loads[0].wait()
    for c in (0, 1):
        pieces(cot, c, snd_c)

    with jax.named_scope("load_space"):
        loads[1].wait()
        loads[2].wait()
        loads[3].wait()

    for f in (0, 1):
        lanes = pl.ds(f * S, S)
        with jax.named_scope("space_qkv"):
            qkv_s[f] = mm_nt(wqs[...], tok[f]).astype(BF)
        with jax.named_scope("space_heads"):
            heads(qkv_s.at[f], None, None, attp_s, lanes)
        with jax.named_scope("space_out"):
            cot[f] = (tok[f].astype(F32) + mm_tn(attp_s[192:768, lanes], wos[...])).astype(BF)
        if f == 0:
            with jax.named_scope("barrier"):
                pl.semaphore_wait(barrier, N - 1)
            exchange(0, 0, snd_c, rcv_c)

    pieces(cot, 0, snd_m)
    exchange(1, 0, snd_m, rcv_m)
    exchange(0, 1, snd_c, rcv_c)
    pieces(cot, 1, snd_m)
    exchange(1, 1, snd_m, rcv_m)

    def sources(code, pair, row):
        gx, gy, gz = code // 16, (code // 4) % 4, code % 4
        return 9 * ((gz % 2) * 64 + gy * 16 + pair * 8 + gx * 2 + gz // 2) + row

    at = lax.broadcasted_iota(jnp.int32, (1024, 1), 0)
    perm[0:1024, :] = jnp.where(
        sources(at // 16, (at // 8) % 2, at % 8) == lax.broadcasted_iota(jnp.int32, (1024, D), 1), 1.0, 0.0).astype(BF)
    at = lax.broadcasted_iota(jnp.int32, (128, 1), 0)
    perm[1024:D, :] = jnp.where(
        sources(at // 2, at % 2, 8) == lax.broadcasted_iota(jnp.int32, (128, D), 1), 1.0, 0.0).astype(BF)
    for ref, row in ((act, 1728), (attp_t, 0), (attp_s, 0)):
        ref[row:row + 192, :] = jnp.zeros((192, 512), BF)
    for f in (0, 1):
        h_s[:, f * S:(f + 1) * S] = mm_nt(perm[...], tok[f]).astype(BF)

    loads[4].wait()
    loads[5].wait()

    @pl.loop(0, 2)
    def _(c):
        lanes = pl.ds(pl.multiple_of(c * S, S), S)
        with jax.named_scope("wait_cotangent"):
            arrived(0, c, snd_c, rcv_c)
        ga_ref[...] = mm_nt(wot[...], rcv_c[c].reshape(S, D)).astype(BF)
        g_t[:, lanes] = mm_nt(perm[...], rcv_c[c].reshape(S, D)).astype(BF)
        with jax.named_scope("wait_hidden"):
            arrived(1, c, snd_m, rcv_m)
        with jax.named_scope("time_qkv"):
            qkv_t[...] = mm_nt(wqt[...], rcv_m[c].reshape(S, D)).astype(BF)
        with jax.named_scope("time_heads"):
            heads(qkv_t, ga_ref, act, attp_t, lanes)
        with jax.named_scope("time_back"):
            up = rcv_c[c].reshape(S, D)
            back = (up.astype(F32) + mm_tn(act[0:1728, lanes], wqt[...])).astype(BF)
            snd_r[c] = back.reshape(128, 2, D)
        with jax.named_scope("time_send"):
            exchange(2, c, snd_r, rcv_r)
        h_t[:, lanes] = mm_nt(perm[...], rcv_m[c].reshape(S, D)).astype(BF)

    def product_of(h_t, attp):
        def product(chunk):
            rows = pl.ds(chunk * LANES, LANES)
            if chunk < 4:
                return mm_nt(h_t[...], act[rows, :])
            right = mm_nt(g_t[...], attp[pl.ds((chunk - 4) * LANES, LANES), :])
            return right + mm_nt(h_t[...], act[rows, :]) if chunk == 4 else right
        return product

    def summed(i, refs, sems):
        return Reduce(where, *refs[0:2], out_m.at[i], out_o.at[i], *refs[2:], *sems)

    time, space = summed(0, time_refs, time_sems), summed(1, space_refs, space_sems)
    with jax.named_scope("time_products"):
        time.start(product_of(h_t, attp_t))
    with jax.named_scope("time_begin"):
        time.begin()

    for c in (0, 1):
        with jax.named_scope("wait_back"):
            arrived(2, c, snd_r, rcv_r)
        both = mm_tn(weave[...], rcv_r[c].reshape(S, D)).astype(BF)
        cot[0, pl.ds(c * 128, 128)] = both[0:128]
        cot[1, pl.ds(c * 128, 128)] = both[128:256]

    for f in (0, 1):
        lanes = pl.ds(f * S, S)
        with jax.named_scope("space_ga"):
            ga_ref[...] = mm_nt(wos[...], cot[f]).astype(BF)
        with jax.named_scope("space_heads_back"):
            heads(qkv_s.at[f], ga_ref, act, None, lanes)
        g_t[:, lanes] = mm_nt(perm[...], cot[f]).astype(BF)
    with jax.named_scope("time_spread"):
        time.spread()
    with jax.named_scope("space_products"):
        space.start(product_of(h_s, attp_s))
    with jax.named_scope("space_begin"):
        space.begin()
    for f in (0, 1):
        with jax.named_scope("space_back"):
            grad_tokens[f] = (cot[f].astype(F32) + mm_tn(act[0:1728, pl.ds(f * S, S)], wqs[...])).astype(BF)
    with jax.named_scope("time_finish"):
        time.finish(gq_time, go_time)
    with jax.named_scope("space_spread"):
        space.spread()
    with jax.named_scope("space_finish"):
        space.finish(gq_space, go_space)

    for kind, (src, dst) in enumerate(((snd_c, rcv_c), (snd_m, rcv_m), (snd_r, rcv_r))):
        for c in (0, 1):
            whole(kind, c, src, dst).wait_send()
    time.drain()
    space.drain()


def hand_over(*refs):
    copies = [pltpu.make_async_copy(refs[i], refs[5 + i], refs[10].at[i]) for i in range(5)]
    for c in copies:
        c.start()
    for c in copies:
        c.wait()


def body(tokens, cotangent, w_qkv_space, w_out_space, w_qkv_time, w_out_time):
    vm = pltpu.VMEM
    pieces = vm((2, N, 2, D), BF)

    def main(n):
        return vm((3, n, 16, LANES), BF)

    def odd(n):
        return vm((3, n, 2, LANES), BF)

    dma = pltpu.SemaphoreType.DMA
    halves = [main(64), odd(64), main(64), odd(64), vm((3, 3, 16, 16, LANES), BF), vm((3, 3, 16, 2, LANES), BF),
              vm((3, 16, 2, 8, LANES), BF), odd(16), vm((3, 32, 8, LANES), BF), odd(32)]
    sums = [dma((3, 4, 2)), dma((3, 4, 2)), dma((2, 3, 2))]
    hbm, inside = pl.BlockSpec(memory_space=pl.ANY), pl.BlockSpec(memory_space=pltpu.VMEM)
    found = pl.pallas_call(
        kernel,
        out_shape=(
            jax.ShapeDtypeStruct((2, S, D), BF),
            jax.ShapeDtypeStruct((9, 1728), F32),
            jax.ShapeDtypeStruct((9, INNER), F32),
            jax.ShapeDtypeStruct((9, 1728), F32),
            jax.ShapeDtypeStruct((9, INNER), F32),
        ),
        in_specs=[hbm] * 6,
        out_specs=(inside,) * 5,
        scratch_shapes=[
            vm((2, S, D), BF), vm((2, S, D), BF), vm((1728, D), BF), vm((INNER, D), BF), vm((1728, D), BF), vm((INNER, D), BF),
            *[pieces] * 6,
            vm((2, 1728, S), BF), vm((1728, S), BF), vm((INNER, S), BF), vm((1920, 512), BF), vm((768, 512), BF), vm((768, 512), BF),
            vm((D, 512), BF), vm((D, 512), BF), vm((D, 512), BF), vm((D, D), BF), vm((S, S), BF),
            vm((2, 3, 64, 16, LANES), BF), vm((2, 3, 64, 2, LANES), BF),
            *halves, *halves,
            dma((6,)), dma((3, 2)), dma((3, 2)), dma((3, 2)), *sums, *sums,
        ],
        compiler_params=pltpu.CompilerParams(
            collective_id=0, has_side_effects=True, vmem_limit_bytes=63 * 2**20),
    )(tokens, cotangent, w_qkv_space.T, w_out_space, w_qkv_time.T, w_out_time)
    grad_tokens, gq_space, go_space, gq_time, go_time = pl.pallas_call(
        hand_over,
        out_shape=tuple(jax.ShapeDtypeStruct(a.shape, a.dtype) for a in found),
        in_specs=[hbm] * 5,
        out_specs=(inside,) * 5,
        scratch_shapes=[dma((5,))],
        compiler_params=pltpu.CompilerParams(vmem_limit_bytes=16 * 2**20),
    )(*found)
    return grad_tokens, gq_space, go_space.T, gq_time, go_time.T


def solution(mesh):
    rows = P(("node", "chip"), None, None)
    return jax.shard_map(
        body,
        mesh=mesh,
        in_specs=(rows, rows, P(), P(), P(), P()),
        out_specs=(rows, P(("node", "chip"), None), P(None, ("node", "chip")),
                   P(("node", "chip"), None), P(None, ("node", "chip"))),
        check_vma=False,
    )
```

```python
import jax
import jax.numpy as jnp
from jax import lax
from jax.experimental import pallas as pl
from jax.experimental.pallas import tpu as pltpu
from jax.sharding import PartitionSpec as P

D = 1152
HEADS = 8
HEAD = 72
INNER = 576
S = 256
N = 128
LANES = 384
F32 = jnp.float32
BF = jnp.bfloat16
MESH = pl.DeviceIdType.MESH
SCALE = HEAD ** (-0.5)
LOG2E = 1.4426950408889634


def place(d):
    return {"node": d // 8, "chip": lax.rem(d, 8)}


def device(x, y, z, core):
    return lax.rem(z, 2) * 64 + y * 16 + core * 8 + x * 2 + z // 2


def mm(a, b):
    return jnp.dot(a, b, preferred_element_type=F32)


def mm_nt(a, b):
    return lax.dot_general(a, b, (((1,), (1,)), ((), ())), preferred_element_type=F32)


def mm_tn(a, b):
    return lax.dot_general(a, b, (((0,), (0,)), ((), ())), preferred_element_type=F32)


def probabilities(q, k):
    e = jnp.exp2(mm_tn(k, q) * (SCALE * LOG2E))
    return e * (1.0 / jnp.sum(e, axis=0, keepdims=True))


def put_pair(ref, row, lanes, two):
    ref[pl.ds(row, 2 * HEAD), lanes] = jnp.concatenate(two, axis=0).astype(BF)


def heads(qkv, ga, act, att, lanes):
    for pair in range(HEADS // 2):
        found = [[], [], [], []]
        for h in (2 * pair, 2 * pair + 1):
            q, k, v = (qkv[pl.ds(i * INNER + h * HEAD, HEAD), :] for i in range(3))
            p = probabilities(q, k)
            low = p.astype(BF)
            if att is not None:
                found[3].append(mm(v, low))
            if act is not None:
                g = ga[pl.ds(h * HEAD, HEAD), :]
                gp = mm_tn(v, g)
                found[2].append(mm_nt(g, low))
                centred = gp - jnp.sum(p * gp, axis=0, keepdims=True)
                gs = (p * centred * SCALE).astype(BF)
                found[0].append(mm(k, gs))
                found[1].append(mm_nt(q, gs))
        if att is not None:
            put_pair(att, 192 + 2 * HEAD * pair, lanes, found[3])
        if act is not None:
            for i in range(3):
                put_pair(act, INNER * i + 2 * HEAD * pair, lanes, found[i])


def turned(b, a):
    return ((b << (2 * a)) | (b >> (6 - 2 * a))) & 63


class Reduce:
    def __init__(self, where, acc, acc_odd, out, out_odd, first, first_odd, near, near_odd, mid, mid_odd, far, far_odd,
                 ssem, rsem, fsem):
        self.where, self.core, self.at = where, where["core"], where["at"]
        self.acc, self.out, self.first = (acc, acc_odd), (out, out_odd), (first, first_odd)
        self.near, self.mid, self.far = (near, near_odd), (mid, mid_odd), (far, far_odd)
        self.ssem, self.rsem, self.fsem = ssem, rsem, fsem

    def copy(self, src, dst, a, step, which, target):
        return pltpu.make_async_remote_copy(
            src_ref=src, dst_ref=dst, send_sem=self.ssem.at[a, step, which], recv_sem=self.rsem.at[a, step, which],
            device_id=target, device_id_type=MESH)

    def core_copies(self, a):
        return [self.copy(self.out[w].at[a], self.first[w].at[a], a, 0, w, self.where["mate"]) for w in (0, 1)]

    def axis_copies(self, a):
        copies = []
        for step in (1, 2, 3):
            to = list(self.at)
            to[a] = lax.rem(to[a] + step, 4)
            block = pl.ds(to[a] * 16, 16)
            copies += [self.copy(self.acc[w].at[a, block], self.near[w].at[a, step - 1], a, step, w,
                                 place(device(*to, self.core))) for w in (0, 1)]
        return copies

    def plane(self, a):
        return self.at[(a + 1) % 3] * 4 + self.at[(a + 2) % 3]

    def plane_copies(self, a, o, k):
        to = list(self.at)
        to[(a + 1) % 3], to[(a + 2) % 3] = o // 4, lax.rem(o, 4)
        slot = self.core * 16 + self.plane(a)
        return [pltpu.make_async_remote_copy(
            src_ref=src, dst_ref=self.far[w].at[a, slot], send_sem=self.fsem.at[0, a, w], recv_sem=self.fsem.at[1, a, w],
            device_id=place(device(*to, k)), device_id_type=MESH)
            for w, src in ((0, self.mid[0].at[a, o, k]), (1, self.mid[1].at[a, o]))]

    def plane_whole(self, a, w):
        part = self.far[w].at[a, pl.ds(0, 31)]
        return pltpu.make_async_remote_copy(
            src_ref=part, dst_ref=part, send_sem=self.fsem.at[0, a, w], recv_sem=self.fsem.at[1, a, w],
            device_id=self.where["mate"], device_id_type=MESH)

    @staticmethod
    def put(value, main, odd, a):
        rows = value[0:1024].reshape(64, 16, LANES).astype(BF)
        rest = value[1024:1152].reshape(64, 2, LANES).astype(BF)
        for b in range(64):
            main[a, turned(b, a)] = rows[b]
            odd[a, turned(b, a)] = rest[b]

    def start(self, product):
        for mine in (0, 1):
            @pl.when(self.core == mine)
            def _():
                for a in (2, 1, 0):
                    self.put(product(3 * (1 - mine) + a), *self.out, a)
                    for c in self.core_copies(a):
                        c.start()
                for a in (2, 1, 0):
                    self.put(product(3 * mine + a), *self.acc, a)

    def begin(self):
        for a in (2, 1, 0):
            for c in self.core_copies(a):
                c.wait_recv()
            for w in (0, 1):
                self.acc[w][a] = self.acc[w][a] + self.first[w][a]
            for c in self.axis_copies(a):
                c.start()

    def spread(self):
        for a in (2, 1, 0):
            for c in self.axis_copies(a):
                c.wait_recv()
            mine = pl.ds(self.at[a] * 16, 16)
            total, rest = (self.acc[w][a, mine].astype(F32) + self.near[w][a, 0].astype(F32)
                           + self.near[w][a, 1].astype(F32) + self.near[w][a, 2].astype(F32) for w in (0, 1))
            self.mid[0][a] = total.reshape(16, 2, 8, LANES).astype(BF)
            self.mid[1][a] = rest.astype(BF)
            here = self.plane(a)
            for c in self.plane_copies(a, here, 1 - self.core):
                c.start()

            @pl.loop(0, 5)
            def _(i):
                for u in range(3):
                    o = lax.rem(here + 1 + i * 3 + u, 16)
                    for k in (0, 1):
                        for c in self.plane_copies(a, o, k):
                            c.start()

    def finish(self, out_qkv, out_out):
        for a in (2, 1, 0):
            for w in (0, 1):
                self.plane_whole(a, w).wait_recv()
            here = self.plane(a)
            self.far[0][a, self.core * 16 + here] = self.mid[0][a, here, self.core]
            self.far[1][a, self.core * 16 + here] = self.mid[1][a, here]
            for half in (0, 1):
                chunk = 3 * half + a
                blocks = pl.ds(half * 16, 16)
                total = jnp.sum(self.far[0][a, blocks].astype(F32), axis=0)
                both = jnp.sum(self.far[1][a, blocks].astype(F32), axis=0)
                for rows, value in ((pl.ds(0, 8), total), (pl.ds(8, 1), jnp.where(self.core == 0, both[0:1], both[1:2]))):
                    if chunk < 4:
                        out_qkv[rows, chunk * LANES:(chunk + 1) * LANES] = value
                    elif chunk == 4:
                        out_qkv[rows, 1536:1728] = value[:, 0:192]
                        out_out[rows, 0:192] = value[:, 192:384]
                    else:
                        out_out[rows, 192:576] = value

    def drain(self):
        for a in range(3):
            for c in self.core_copies(a) + self.axis_copies(a):
                c.wait_send()
            for w in (0, 1):
                self.plane_whole(a, w).wait_send()


def kernel(tokens, cotangent, w_qkv_space, w_out_space, w_qkv_time, w_out_time,
           grad_tokens, gq_space, go_space, gq_time, go_time,
           tok, cot, wqs, wos, wqt, wot,
           snd_c, rcv_c, snd_m, rcv_m, snd_r, rcv_r,
           qkv_s, qkv_t, ga_ref, act, attp_t, attp_s, h_t, g_t, h_s, perm, weave, out_m, out_o, *rest):
    time_refs, space_refs = rest[0:10], rest[10:20]
    load_sem, local_sem, a2a_send, a2a_recv = rest[20:24]
    time_sems, space_sems = rest[24:27], rest[27:30]
    node, chip = lax.axis_index("node"), lax.axis_index("chip")
    me = node * 8 + chip
    barrier = pltpu.get_barrier_semaphore()

    def others(body):
        @pl.loop(0, 18)
        def _(i):
            for u in range(7):
                body(lax.rem(me + 1 + i * 7 + u, N))
        body(lax.rem(me + 127, N))

    others(lambda d: pl.semaphore_signal(barrier, inc=1, device_id=place(d), device_id_type=MESH))

    loads = [pltpu.make_async_copy(src, dst, load_sem.at[i]) for i, (src, dst) in enumerate(
        ((cotangent, cot), (tokens, tok), (w_qkv_space, wqs), (w_out_space, wos), (w_qkv_time, wqt), (w_out_time, wot)))]
    for c in loads:
        c.start()

    core = lax.rem(node, 2)
    x, y, z = chip // 2, lax.rem(node // 2, 4), lax.rem(chip, 2) * 2 + node // 8

    where = {"core": core, "at": (x, y, z), "mate": place(device(x, y, z, 1 - core))}

    to = lax.broadcasted_iota(jnp.int32, (S, S), 0)
    fro = lax.broadcasted_iota(jnp.int32, (S, S), 1)
    weave[...] = jnp.where((to % 2) * 128 + to // 2 == fro, 1.0, 0.0).astype(BF)

    def pieces(rows_of, c, dst):
        both = jnp.concatenate([rows_of[0, pl.ds(c * 128, 128)], rows_of[1, pl.ds(c * 128, 128)]], axis=0)
        dst[c] = mm(weave[...], both).astype(BF).reshape(128, 2, D)

    def exchange(kind, c, src, dst):
        pltpu.make_async_copy(src.at[c, me], dst.at[c, me], local_sem.at[kind, c]).start()
        others(lambda d: pltpu.make_async_remote_copy(
            src_ref=src.at[c, d], dst_ref=dst.at[c, me], send_sem=a2a_send.at[kind, c], recv_sem=a2a_recv.at[kind, c],
            device_id=place(d), device_id_type=MESH).start())

    def whole(kind, c, src, dst):
        return pltpu.make_async_remote_copy(
            src_ref=src.at[c, pl.ds(0, N - 1)], dst_ref=dst.at[c, pl.ds(0, N - 1)], send_sem=a2a_send.at[kind, c],
            recv_sem=a2a_recv.at[kind, c], device_id=where["mate"], device_id_type=MESH)

    def arrived(kind, c, src, dst):
        whole(kind, c, src, dst).wait_recv()
        pltpu.make_async_copy(src.at[c, me], dst.at[c, me], local_sem.at[kind, c]).wait()

    with jax.named_scope("load_cotangent"):
        loads[0].wait()
    for c in (0, 1):
        pieces(cot, c, snd_c)

    with jax.named_scope("load_space"):
        loads[1].wait()
        loads[2].wait()
        loads[3].wait()

    for f in (0, 1):
        lanes = pl.ds(f * S, S)
        with jax.named_scope("space_qkv"):
            qkv_s[f] = mm_nt(wqs[...], tok[f]).astype(BF)
        with jax.named_scope("space_heads"):
            heads(qkv_s.at[f], None, None, attp_s, lanes)
        with jax.named_scope("space_out"):
            cot[f] = (tok[f].astype(F32) + mm_tn(attp_s[192:768, lanes], wos[...])).astype(BF)
        if f == 0:
            with jax.named_scope("barrier"):
                pl.semaphore_wait(barrier, N - 1)
            exchange(0, 0, snd_c, rcv_c)

    pieces(cot, 0, snd_m)
    exchange(1, 0, snd_m, rcv_m)
    exchange(0, 1, snd_c, rcv_c)
    pieces(cot, 1, snd_m)
    exchange(1, 1, snd_m, rcv_m)

    def sources(code, pair, row):
        gx, gy, gz = code // 16, (code // 4) % 4, code % 4
        return 9 * ((gz % 2) * 64 + gy * 16 + pair * 8 + gx * 2 + gz // 2) + row

    at = lax.broadcasted_iota(jnp.int32, (1024, 1), 0)
    perm[0:1024, :] = jnp.where(
        sources(at // 16, (at // 8) % 2, at % 8) == lax.broadcasted_iota(jnp.int32, (1024, D), 1), 1.0, 0.0).astype(BF)
    at = lax.broadcasted_iota(jnp.int32, (128, 1), 0)
    perm[1024:D, :] = jnp.where(
        sources(at // 2, at % 2, 8) == lax.broadcasted_iota(jnp.int32, (128, D), 1), 1.0, 0.0).astype(BF)
    for ref, row in ((act, 1728), (attp_t, 0), (attp_s, 0)):
        ref[row:row + 192, :] = jnp.zeros((192, 512), BF)
    for f in (0, 1):
        h_s[:, f * S:(f + 1) * S] = mm_nt(perm[...], tok[f]).astype(BF)

    loads[4].wait()
    loads[5].wait()

    @pl.loop(0, 2)
    def _(c):
        lanes = pl.ds(pl.multiple_of(c * S, S), S)
        with jax.named_scope("wait_cotangent"):
            arrived(0, c, snd_c, rcv_c)
        ga_ref[...] = mm_nt(wot[...], rcv_c[c].reshape(S, D)).astype(BF)
        g_t[:, lanes] = mm_nt(perm[...], rcv_c[c].reshape(S, D)).astype(BF)
        with jax.named_scope("wait_hidden"):
            arrived(1, c, snd_m, rcv_m)
        with jax.named_scope("time_qkv"):
            qkv_t[...] = mm_nt(wqt[...], rcv_m[c].reshape(S, D)).astype(BF)
        with jax.named_scope("time_heads"):
            heads(qkv_t, ga_ref, act, attp_t, lanes)
        with jax.named_scope("time_back"):
            up = rcv_c[c].reshape(S, D)
            back = (up.astype(F32) + mm_tn(act[0:1728, lanes], wqt[...])).astype(BF)
            snd_r[c] = back.reshape(128, 2, D)
        with jax.named_scope("time_send"):
            exchange(2, c, snd_r, rcv_r)
        h_t[:, lanes] = mm_nt(perm[...], rcv_m[c].reshape(S, D)).astype(BF)

    def product_of(h_t, attp):
        def product(chunk):
            rows = pl.ds(chunk * LANES, LANES)
            if chunk < 4:
                return mm_nt(h_t[...], act[rows, :])
            right = mm_nt(g_t[...], attp[pl.ds((chunk - 4) * LANES, LANES), :])
            return right + mm_nt(h_t[...], act[rows, :]) if chunk == 4 else right
        return product

    def summed(i, refs, sems):
        return Reduce(where, *refs[0:2], out_m.at[i], out_o.at[i], *refs[2:], *sems)

    time, space = summed(0, time_refs, time_sems), summed(1, space_refs, space_sems)
    with jax.named_scope("time_products"):
        time.start(product_of(h_t, attp_t))
    with jax.named_scope("time_begin"):
        time.begin()

    for c in (0, 1):
        with jax.named_scope("wait_back"):
            arrived(2, c, snd_r, rcv_r)
        both = mm_tn(weave[...], rcv_r[c].reshape(S, D)).astype(BF)
        cot[0, pl.ds(c * 128, 128)] = both[0:128]
        cot[1, pl.ds(c * 128, 128)] = both[128:256]

    for f in (0, 1):
        lanes = pl.ds(f * S, S)
        with jax.named_scope("space_ga"):
            ga_ref[...] = mm_nt(wos[...], cot[f]).astype(BF)
        with jax.named_scope("space_heads_back"):
            heads(qkv_s.at[f], ga_ref, act, None, lanes)
        g_t[:, lanes] = mm_nt(perm[...], cot[f]).astype(BF)
    with jax.named_scope("time_spread"):
        time.spread()
    with jax.named_scope("space_products"):
        space.start(product_of(h_s, attp_s))
    with jax.named_scope("space_begin"):
        space.begin()
    for f in (0, 1):
        with jax.named_scope("space_back"):
            grad_tokens[f] = (cot[f].astype(F32) + mm_tn(act[0:1728, pl.ds(f * S, S)], wqs[...])).astype(BF)
    with jax.named_scope("time_finish"):
        time.finish(gq_time, go_time)
    with jax.named_scope("space_spread"):
        space.spread()
    with jax.named_scope("space_finish"):
        space.finish(gq_space, go_space)

    for kind, (src, dst) in enumerate(((snd_c, rcv_c), (snd_m, rcv_m), (snd_r, rcv_r))):
        for c in (0, 1):
            whole(kind, c, src, dst).wait_send()
    time.drain()
    space.drain()


def hand_over(*refs):
    copies = [pltpu.make_async_copy(refs[i], refs[5 + i], refs[10].at[i]) for i in range(5)]
    for c in copies:
        c.start()
    for c in copies:
        c.wait()


def body(tokens, cotangent, w_qkv_space, w_out_space, w_qkv_time, w_out_time):
    vm = pltpu.VMEM
    pieces = vm((2, N, 2, D), BF)

    def main(n):
        return vm((3, n, 16, LANES), BF)

    def odd(n):
        return vm((3, n, 2, LANES), BF)

    dma = pltpu.SemaphoreType.DMA
    halves = [main(64), odd(64), main(64), odd(64), vm((3, 3, 16, 16, LANES), BF), vm((3, 3, 16, 2, LANES), BF),
              vm((3, 16, 2, 8, LANES), BF), odd(16), vm((3, 32, 8, LANES), BF), odd(32)]
    sums = [dma((3, 4, 2)), dma((3, 4, 2)), dma((2, 3, 2))]
    hbm, inside = pl.BlockSpec(memory_space=pl.ANY), pl.BlockSpec(memory_space=pltpu.VMEM)
    found = pl.pallas_call(
        kernel,
        out_shape=(
            jax.ShapeDtypeStruct((2, S, D), BF),
            jax.ShapeDtypeStruct((9, 1728), F32),
            jax.ShapeDtypeStruct((9, INNER), F32),
            jax.ShapeDtypeStruct((9, 1728), F32),
            jax.ShapeDtypeStruct((9, INNER), F32),
        ),
        in_specs=[hbm] * 6,
        out_specs=(inside,) * 5,
        scratch_shapes=[
            vm((2, S, D), BF), vm((2, S, D), BF), vm((1728, D), BF), vm((INNER, D), BF), vm((1728, D), BF), vm((INNER, D), BF),
            *[pieces] * 6,
            vm((2, 1728, S), BF), vm((1728, S), BF), vm((INNER, S), BF), vm((1920, 512), BF), vm((768, 512), BF), vm((768, 512), BF),
            vm((D, 512), BF), vm((D, 512), BF), vm((D, 512), BF), vm((D, D), BF), vm((S, S), BF),
            vm((2, 3, 64, 16, LANES), BF), vm((2, 3, 64, 2, LANES), BF),
            *halves, *halves,
            dma((6,)), dma((3, 2)), dma((3, 2)), dma((3, 2)), *sums, *sums,
        ],
        compiler_params=pltpu.CompilerParams(
            collective_id=0, has_side_effects=True, vmem_limit_bytes=63 * 2**20),
    )(tokens, cotangent, w_qkv_space.T, w_out_space, w_qkv_time.T, w_out_time)
    grad_tokens, gq_space, go_space, gq_time, go_time = pl.pallas_call(
        hand_over,
        out_shape=tuple(jax.ShapeDtypeStruct(a.shape, a.dtype) for a in found),
        in_specs=[hbm] * 5,
        out_specs=(inside,) * 5,
        scratch_shapes=[dma((5,))],
        compiler_params=pltpu.CompilerParams(vmem_limit_bytes=63 * 2**20),
    )(*found)
    return grad_tokens, gq_space, go_space.T, gq_time, go_time.T


def solution(mesh):
    rows = P(("node", "chip"), None, None)
    return jax.shard_map(
        body,
        mesh=mesh,
        in_specs=(rows, rows, P(), P(), P(), P()),
        out_specs=(rows, P(("node", "chip"), None), P(None, ("node", "chip")),
                   P(("node", "chip"), None), P(None, ("node", "chip"))),
        check_vma=False,
    )
```

```python
import jax
import jax.numpy as jnp
from jax import lax
from jax.experimental import pallas as pl
from jax.experimental.pallas import tpu as pltpu
from jax.sharding import PartitionSpec as P

D = 1152
HEADS = 8
HEAD = 72
INNER = 576
S = 256
N = 128
LANES = 384
F32 = jnp.float32
BF = jnp.bfloat16
MESH = pl.DeviceIdType.MESH
SCALE = HEAD ** (-0.5)
LOG2E = 1.4426950408889634


def place(d):
    return {"node": d // 8, "chip": lax.rem(d, 8)}


def device(x, y, z, core):
    return lax.rem(z, 2) * 64 + y * 16 + core * 8 + x * 2 + z // 2


def mm(a, b):
    return jnp.dot(a, b, preferred_element_type=F32)


def mm_nt(a, b):
    return lax.dot_general(a, b, (((1,), (1,)), ((), ())), preferred_element_type=F32)


def mm_tn(a, b):
    return lax.dot_general(a, b, (((0,), (0,)), ((), ())), preferred_element_type=F32)


def probabilities(q, k):
    e = jnp.exp2(mm_tn(k, q) * (SCALE * LOG2E))
    return e * (1.0 / jnp.sum(e, axis=0, keepdims=True))


def put_pair(ref, row, lanes, two):
    ref[pl.ds(row, 2 * HEAD), lanes] = jnp.concatenate(two, axis=0).astype(BF)


def heads(qkv, ga, act, att, lanes):
    for pair in range(HEADS // 2):
        found = [[], [], [], []]
        for h in (2 * pair, 2 * pair + 1):
            q, k, v = (qkv[pl.ds(i * INNER + h * HEAD, HEAD), :] for i in range(3))
            p = probabilities(q, k)
            low = p.astype(BF)
            if att is not None:
                found[3].append(mm(v, low))
            if act is not None:
                g = ga[pl.ds(h * HEAD, HEAD), :]
                gp = mm_tn(v, g)
                found[2].append(mm_nt(g, low))
                centred = gp - jnp.sum(p * gp, axis=0, keepdims=True)
                gs = (p * centred * SCALE).astype(BF)
                found[0].append(mm(k, gs))
                found[1].append(mm_nt(q, gs))
        if att is not None:
            put_pair(att, 192 + 2 * HEAD * pair, lanes, found[3])
        if act is not None:
            for i in range(3):
                put_pair(act, INNER * i + 2 * HEAD * pair, lanes, found[i])


def turned(b, a):
    return ((b << (2 * a)) | (b >> (6 - 2 * a))) & 63


class Reduce:
    def __init__(self, where, acc, acc_odd, out, out_odd, first, first_odd, near, near_odd, mid, mid_odd, far, far_odd,
                 ssem, rsem, fsem):
        self.where, self.core, self.at = where, where["core"], where["at"]
        self.acc, self.out, self.first = (acc, acc_odd), (out, out_odd), (first, first_odd)
        self.near, self.mid, self.far = (near, near_odd), (mid, mid_odd), (far, far_odd)
        self.ssem, self.rsem, self.fsem = ssem, rsem, fsem

    def copy(self, src, dst, a, step, which, target):
        return pltpu.make_async_remote_copy(
            src_ref=src, dst_ref=dst, send_sem=self.ssem.at[a, step, which], recv_sem=self.rsem.at[a, step, which],
            device_id=target, device_id_type=MESH)

    def core_copies(self, a):
        return [self.copy(self.out[w].at[a], self.first[w].at[a], a, 0, w, self.where["mate"]) for w in (0, 1)]

    def axis_copies(self, a):
        copies = []
        for step in (1, 2, 3):
            to = list(self.at)
            to[a] = lax.rem(to[a] + step, 4)
            block = pl.ds(to[a] * 16, 16)
            copies += [self.copy(self.acc[w].at[a, block], self.near[w].at[a, step - 1], a, step, w,
                                 place(device(*to, self.core))) for w in (0, 1)]
        return copies

    def plane(self, a):
        return self.at[(a + 1) % 3] * 4 + self.at[(a + 2) % 3]

    def plane_copies(self, a, o, k):
        to = list(self.at)
        to[(a + 1) % 3], to[(a + 2) % 3] = o // 4, lax.rem(o, 4)
        slot = self.core * 16 + self.plane(a)
        return [pltpu.make_async_remote_copy(
            src_ref=src, dst_ref=self.far[w].at[a, slot], send_sem=self.fsem.at[0, a, w], recv_sem=self.fsem.at[1, a, w],
            device_id=place(device(*to, k)), device_id_type=MESH)
            for w, src in ((0, self.mid[0].at[a, o, k]), (1, self.mid[1].at[a, o]))]

    def plane_whole(self, a, w):
        part = self.far[w].at[a, pl.ds(0, 31)]
        return pltpu.make_async_remote_copy(
            src_ref=part, dst_ref=part, send_sem=self.fsem.at[0, a, w], recv_sem=self.fsem.at[1, a, w],
            device_id=self.where["mate"], device_id_type=MESH)

    @staticmethod
    def put(value, main, odd, a):
        rows = value[0:1024].reshape(64, 16, LANES).astype(BF)
        rest = value[1024:1152].reshape(64, 2, LANES).astype(BF)
        for b in range(64):
            main[a, turned(b, a)] = rows[b]
            odd[a, turned(b, a)] = rest[b]

    def start(self, product):
        for mine in (0, 1):
            @pl.when(self.core == mine)
            def _():
                for a in (2, 1, 0):
                    self.put(product(3 * (1 - mine) + a), *self.out, a)
                    for c in self.core_copies(a):
                        c.start()
                for a in (2, 1, 0):
                    self.put(product(3 * mine + a), *self.acc, a)

    def begin(self):
        for a in (2, 1, 0):
            for c in self.core_copies(a):
                c.wait_recv()
            for w in (0, 1):
                self.acc[w][a] = self.acc[w][a] + self.first[w][a]
            for c in self.axis_copies(a):
                c.start()

    def spread(self):
        for a in (2, 1, 0):
            for c in self.axis_copies(a):
                c.wait_recv()
            mine = pl.ds(self.at[a] * 16, 16)
            total, rest = (self.acc[w][a, mine].astype(F32) + self.near[w][a, 0].astype(F32)
                           + self.near[w][a, 1].astype(F32) + self.near[w][a, 2].astype(F32) for w in (0, 1))
            self.mid[0][a] = total.reshape(16, 2, 8, LANES).astype(BF)
            self.mid[1][a] = rest.astype(BF)
            here = self.plane(a)
            for c in self.plane_copies(a, here, 1 - self.core):
                c.start()

            @pl.loop(0, 5)
            def _(i):
                for u in range(3):
                    o = lax.rem(here + 1 + i * 3 + u, 16)
                    for k in (0, 1):
                        for c in self.plane_copies(a, o, k):
                            c.start()

    def finish(self, out_qkv, out_out):
        for a in (2, 1, 0):
            for w in (0, 1):
                self.plane_whole(a, w).wait_recv()
            here = self.plane(a)
            self.far[0][a, self.core * 16 + here] = self.mid[0][a, here, self.core]
            self.far[1][a, self.core * 16 + here] = self.mid[1][a, here]
            for half in (0, 1):
                chunk = 3 * half + a
                blocks = pl.ds(half * 16, 16)
                total = jnp.sum(self.far[0][a, blocks].astype(F32), axis=0)
                both = jnp.sum(self.far[1][a, blocks].astype(F32), axis=0)
                for rows, value in ((pl.ds(0, 8), total), (pl.ds(8, 1), jnp.where(self.core == 0, both[0:1], both[1:2]))):
                    if chunk < 4:
                        out_qkv[rows, chunk * LANES:(chunk + 1) * LANES] = value
                    elif chunk == 4:
                        out_qkv[rows, 1536:1728] = value[:, 0:192]
                        out_out[rows, 0:192] = value[:, 192:384]
                    else:
                        out_out[rows, 192:576] = value

    def drain(self):
        for a in range(3):
            for c in self.core_copies(a) + self.axis_copies(a):
                c.wait_send()
            for w in (0, 1):
                self.plane_whole(a, w).wait_send()


def kernel(tokens, cotangent, w_qkv_space, w_out_space, w_qkv_time, w_out_time,
           grad_tokens, gq_space, go_space, gq_time, go_time,
           tok, cot, wqs, wos, wqt, wot,
           snd_c, rcv_c, snd_m, rcv_m, snd_r, rcv_r,
           qkv_s, qkv_t, ga_ref, act, attp_t, attp_s, h_t, g_t, h_s, perm, weave, out_m, out_o, *rest):
    time_refs, space_refs = rest[0:10], rest[10:20]
    load_sem, local_sem, a2a_send, a2a_recv = rest[20:24]
    time_sems, space_sems = rest[24:27], rest[27:30]
    node, chip = lax.axis_index("node"), lax.axis_index("chip")
    me = node * 8 + chip
    barrier = pltpu.get_barrier_semaphore()

    def others(body):
        @pl.loop(0, 18)
        def _(i):
            for u in range(7):
                body(lax.rem(me + 1 + i * 7 + u, N))
        body(lax.rem(me + 127, N))

    others(lambda d: pl.semaphore_signal(barrier, inc=1, device_id=place(d), device_id_type=MESH))

    loads = [pltpu.make_async_copy(src, dst, load_sem.at[i]) for i, (src, dst) in enumerate(
        ((cotangent, cot), (tokens, tok), (w_qkv_space, wqs), (w_out_space, wos), (w_qkv_time, wqt), (w_out_time, wot)))]
    for c in loads:
        c.start()

    core = lax.rem(node, 2)
    x, y, z = chip // 2, lax.rem(node // 2, 4), lax.rem(chip, 2) * 2 + node // 8

    where = {"core": core, "at": (x, y, z), "mate": place(device(x, y, z, 1 - core))}

    to = lax.broadcasted_iota(jnp.int32, (S, S), 0)
    fro = lax.broadcasted_iota(jnp.int32, (S, S), 1)
    weave[...] = jnp.where((to % 2) * 128 + to // 2 == fro, 1.0, 0.0).astype(BF)

    def pieces(rows_of, c, dst):
        both = jnp.concatenate([rows_of[0, pl.ds(c * 128, 128)], rows_of[1, pl.ds(c * 128, 128)]], axis=0)
        dst[c] = mm(weave[...], both).astype(BF).reshape(128, 2, D)

    def exchange(kind, c, src, dst):
        pltpu.make_async_copy(src.at[c, me], dst.at[c, me], local_sem.at[kind, c]).start()
        others(lambda d: pltpu.make_async_remote_copy(
            src_ref=src.at[c, d], dst_ref=dst.at[c, me], send_sem=a2a_send.at[kind, c], recv_sem=a2a_recv.at[kind, c],
            device_id=place(d), device_id_type=MESH).start())

    def whole(kind, c, src, dst):
        return pltpu.make_async_remote_copy(
            src_ref=src.at[c, pl.ds(0, N - 1)], dst_ref=dst.at[c, pl.ds(0, N - 1)], send_sem=a2a_send.at[kind, c],
            recv_sem=a2a_recv.at[kind, c], device_id=where["mate"], device_id_type=MESH)

    def arrived(kind, c, src, dst):
        whole(kind, c, src, dst).wait_recv()
        pltpu.make_async_copy(src.at[c, me], dst.at[c, me], local_sem.at[kind, c]).wait()

    with jax.named_scope("load_cotangent"):
        loads[0].wait()
    for c in (0, 1):
        pieces(cot, c, snd_c)

    with jax.named_scope("load_space"):
        loads[1].wait()
        loads[2].wait()
        loads[3].wait()

    for f in (0, 1):
        lanes = pl.ds(f * S, S)
        with jax.named_scope("space_qkv"):
            qkv_s[f] = mm_nt(wqs[...], tok[f]).astype(BF)
        with jax.named_scope("space_heads"):
            heads(qkv_s.at[f], None, None, attp_s, lanes)
        with jax.named_scope("space_out"):
            cot[f] = (tok[f].astype(F32) + mm_tn(attp_s[192:768, lanes], wos[...])).astype(BF)
        if f == 0:
            with jax.named_scope("barrier"):
                pl.semaphore_wait(barrier, N - 1)
            exchange(0, 0, snd_c, rcv_c)

    pieces(cot, 0, snd_m)
    exchange(1, 0, snd_m, rcv_m)
    exchange(0, 1, snd_c, rcv_c)
    pieces(cot, 1, snd_m)
    exchange(1, 1, snd_m, rcv_m)

    def sources(code, pair, row):
        gx, gy, gz = code // 16, (code // 4) % 4, code % 4
        return 9 * ((gz % 2) * 64 + gy * 16 + pair * 8 + gx * 2 + gz // 2) + row

    at = lax.broadcasted_iota(jnp.int32, (1024, 1), 0)
    perm[0:1024, :] = jnp.where(
        sources(at // 16, (at // 8) % 2, at % 8) == lax.broadcasted_iota(jnp.int32, (1024, D), 1), 1.0, 0.0).astype(BF)
    at = lax.broadcasted_iota(jnp.int32, (128, 1), 0)
    perm[1024:D, :] = jnp.where(
        sources(at // 2, at % 2, 8) == lax.broadcasted_iota(jnp.int32, (128, D), 1), 1.0, 0.0).astype(BF)
    for ref, row in ((act, 1728), (attp_t, 0), (attp_s, 0)):
        ref[row:row + 192, :] = jnp.zeros((192, 512), BF)
    for f in (0, 1):
        h_s[:, f * S:(f + 1) * S] = mm_nt(perm[...], tok[f]).astype(BF)

    sides = [jnp.concatenate([attp_s[:, c * 128:(c + 1) * 128], attp_s[:, S + c * 128:S + (c + 1) * 128]], axis=1) for c in (0, 1)]
    for c in (0, 1):
        attp_s[:, c * S:(c + 1) * S] = mm_nt(sides[c], weave[...]).astype(BF)

    loads[4].wait()
    loads[5].wait()

    @pl.loop(0, 2)
    def _(c):
        lanes = pl.ds(pl.multiple_of(c * S, S), S)
        with jax.named_scope("wait_cotangent"):
            arrived(0, c, snd_c, rcv_c)
        ga_ref[...] = mm_nt(wot[...], rcv_c[c].reshape(S, D)).astype(BF)
        with jax.named_scope("wait_hidden"):
            arrived(1, c, snd_m, rcv_m)
        with jax.named_scope("time_qkv"):
            qkv_t[...] = mm_nt(wqt[...], rcv_m[c].reshape(S, D)).astype(BF)
        with jax.named_scope("time_heads"):
            heads(qkv_t, ga_ref, act, attp_t, lanes)
        with jax.named_scope("time_back"):
            up = rcv_c[c].reshape(S, D)
            back = (up.astype(F32) + mm_tn(act[0:1728, lanes], wqt[...])).astype(BF)
            snd_r[c] = back.reshape(128, 2, D)
        with jax.named_scope("time_send"):
            exchange(2, c, snd_r, rcv_r)

    for c in (0, 1):
        h_t[:, c * S:(c + 1) * S] = mm_nt(perm[...], rcv_m[c].reshape(S, D)).astype(BF)
        g_t[:, c * S:(c + 1) * S] = mm_nt(perm[...], rcv_c[c].reshape(S, D)).astype(BF)

    def product_of(h_t, attp):
        def product(chunk):
            rows = pl.ds(chunk * LANES, LANES)
            if chunk < 4:
                return mm_nt(h_t[...], act[rows, :])
            right = mm_nt(g_t[...], attp[pl.ds((chunk - 4) * LANES, LANES), :])
            return right + mm_nt(h_t[...], act[rows, :]) if chunk == 4 else right
        return product

    def summed(i, refs, sems):
        return Reduce(where, *refs[0:2], out_m.at[i], out_o.at[i], *refs[2:], *sems)

    time, space = summed(0, time_refs, time_sems), summed(1, space_refs, space_sems)
    with jax.named_scope("time_products"):
        time.start(product_of(h_t, attp_t))
    with jax.named_scope("time_begin"):
        time.begin()

    for c in (0, 1):
        with jax.named_scope("wait_back"):
            arrived(2, c, snd_r, rcv_r)
        g_t[:, c * S:(c + 1) * S] = mm_nt(perm[...], rcv_r[c].reshape(S, D)).astype(BF)
        both = mm_tn(weave[...], rcv_r[c].reshape(S, D)).astype(BF)
        cot[0, pl.ds(c * 128, 128)] = both[0:128]
        cot[1, pl.ds(c * 128, 128)] = both[128:256]

    for f in (0, 1):
        lanes = pl.ds(f * S, S)
        with jax.named_scope("space_ga"):
            ga_ref[...] = mm_nt(wos[...], cot[f]).astype(BF)
        with jax.named_scope("space_heads_back"):
            heads(qkv_s.at[f], ga_ref, act, None, lanes)
    with jax.named_scope("time_spread"):
        time.spread()
    with jax.named_scope("space_products"):
        space.start(product_of(h_s, attp_s))
    with jax.named_scope("space_begin"):
        space.begin()
    for f in (0, 1):
        with jax.named_scope("space_back"):
            grad_tokens[f] = (cot[f].astype(F32) + mm_tn(act[0:1728, pl.ds(f * S, S)], wqs[...])).astype(BF)
    with jax.named_scope("time_finish"):
        time.finish(gq_time, go_time)
    with jax.named_scope("space_spread"):
        space.spread()
    with jax.named_scope("space_finish"):
        space.finish(gq_space, go_space)

    for kind, (src, dst) in enumerate(((snd_c, rcv_c), (snd_m, rcv_m), (snd_r, rcv_r))):
        for c in (0, 1):
            whole(kind, c, src, dst).wait_send()
    time.drain()
    space.drain()


def hand_over(*refs):
    copies = [pltpu.make_async_copy(refs[i], refs[5 + i], refs[10].at[i]) for i in range(5)]
    for c in copies:
        c.start()
    for c in copies:
        c.wait()


def body(tokens, cotangent, w_qkv_space, w_out_space, w_qkv_time, w_out_time):
    vm = pltpu.VMEM
    pieces = vm((2, N, 2, D), BF)

    def main(n):
        return vm((3, n, 16, LANES), BF)

    def odd(n):
        return vm((3, n, 2, LANES), BF)

    dma = pltpu.SemaphoreType.DMA
    halves = [main(64), odd(64), main(64), odd(64), vm((3, 3, 16, 16, LANES), BF), vm((3, 3, 16, 2, LANES), BF),
              vm((3, 16, 2, 8, LANES), BF), odd(16), vm((3, 32, 8, LANES), BF), odd(32)]
    sums = [dma((3, 4, 2)), dma((3, 4, 2)), dma((2, 3, 2))]
    hbm, inside = pl.BlockSpec(memory_space=pl.ANY), pl.BlockSpec(memory_space=pltpu.VMEM)
    found = pl.pallas_call(
        kernel,
        out_shape=(
            jax.ShapeDtypeStruct((2, S, D), BF),
            jax.ShapeDtypeStruct((9, 1728), F32),
            jax.ShapeDtypeStruct((9, INNER), F32),
            jax.ShapeDtypeStruct((9, 1728), F32),
            jax.ShapeDtypeStruct((9, INNER), F32),
        ),
        in_specs=[hbm] * 6,
        out_specs=(inside,) * 5,
        scratch_shapes=[
            vm((2, S, D), BF), vm((2, S, D), BF), vm((1728, D), BF), vm((INNER, D), BF), vm((1728, D), BF), vm((INNER, D), BF),
            *[pieces] * 6,
            vm((2, 1728, S), BF), vm((1728, S), BF), vm((INNER, S), BF), vm((1920, 512), BF), vm((768, 512), BF), vm((768, 512), BF),
            vm((D, 512), BF), vm((D, 512), BF), vm((D, 512), BF), vm((D, D), BF), vm((S, S), BF),
            vm((2, 3, 64, 16, LANES), BF), vm((2, 3, 64, 2, LANES), BF),
            *halves, *halves,
            dma((6,)), dma((3, 2)), dma((3, 2)), dma((3, 2)), *sums, *sums,
        ],
        compiler_params=pltpu.CompilerParams(
            collective_id=0, has_side_effects=True, vmem_limit_bytes=63 * 2**20),
    )(tokens, cotangent, w_qkv_space.T, w_out_space, w_qkv_time.T, w_out_time)
    grad_tokens, gq_space, go_space, gq_time, go_time = pl.pallas_call(
        hand_over,
        out_shape=tuple(jax.ShapeDtypeStruct(a.shape, a.dtype) for a in found),
        in_specs=[hbm] * 5,
        out_specs=(inside,) * 5,
        scratch_shapes=[dma((5,))],
        compiler_params=pltpu.CompilerParams(vmem_limit_bytes=63 * 2**20),
    )(*found)
    return grad_tokens, gq_space, go_space.T, gq_time, go_time.T


def solution(mesh):
    rows = P(("node", "chip"), None, None)
    return jax.shard_map(
        body,
        mesh=mesh,
        in_specs=(rows, rows, P(), P(), P(), P()),
        out_specs=(rows, P(("node", "chip"), None), P(None, ("node", "chip")),
                   P(("node", "chip"), None), P(None, ("node", "chip"))),
        check_vma=False,
    )
```

```python
import jax
import jax.numpy as jnp
from jax import lax
from jax.experimental import pallas as pl
from jax.experimental.pallas import tpu as pltpu
from jax.sharding import PartitionSpec as P

D = 1152
HEADS = 8
HEAD = 72
INNER = 576
S = 256
N = 128
LANES = 384
F32 = jnp.float32
BF = jnp.bfloat16
MESH = pl.DeviceIdType.MESH
SCALE = HEAD ** (-0.5)
LOG2E = 1.4426950408889634


def place(d):
    return {"node": d // 8, "chip": lax.rem(d, 8)}


def device(x, y, z, core):
    return lax.rem(z, 2) * 64 + y * 16 + core * 8 + x * 2 + z // 2


def mm(a, b):
    return jnp.dot(a, b, preferred_element_type=F32)


def mm_nt(a, b):
    return lax.dot_general(a, b, (((1,), (1,)), ((), ())), preferred_element_type=F32)


def mm_tn(a, b):
    return lax.dot_general(a, b, (((0,), (0,)), ((), ())), preferred_element_type=F32)


def probabilities(q, k):
    e = jnp.exp2(mm_tn(k, q) * (SCALE * LOG2E))
    return e * (1.0 / jnp.sum(e, axis=0, keepdims=True))


def put_pair(ref, row, lanes, two):
    ref[pl.ds(row, 2 * HEAD), lanes] = jnp.concatenate(two, axis=0).astype(BF)


def heads(qkv, ga, act, att, lanes):
    for pair in range(HEADS // 2):
        found = [[], [], [], []]
        for h in (2 * pair, 2 * pair + 1):
            q, k, v = (qkv[pl.ds(i * INNER + h * HEAD, HEAD), :] for i in range(3))
            p = probabilities(q, k)
            low = p.astype(BF)
            if att is not None:
                found[3].append(mm(v, low))
            if act is not None:
                g = ga[pl.ds(h * HEAD, HEAD), :]
                gp = mm_tn(v, g)
                found[2].append(mm_nt(g, low))
                centred = gp - jnp.sum(p * gp, axis=0, keepdims=True)
                gs = (p * centred * SCALE).astype(BF)
                found[0].append(mm(k, gs))
                found[1].append(mm_nt(q, gs))
        if att is not None:
            put_pair(att, 192 + 2 * HEAD * pair, lanes, found[3])
        if act is not None:
            for i in range(3):
                put_pair(act, INNER * i + 2 * HEAD * pair, lanes, found[i])


def turned(b, a):
    return ((b << (2 * a)) | (b >> (6 - 2 * a))) & 63


class Reduce:
    def __init__(self, where, acc, acc_odd, out, out_odd, first, first_odd, near, near_odd, mid, mid_odd, far, far_odd,
                 ssem, rsem, fsem):
        self.where, self.core, self.at = where, where["core"], where["at"]
        self.acc, self.out, self.first = (acc, acc_odd), (out, out_odd), (first, first_odd)
        self.near, self.mid, self.far = (near, near_odd), (mid, mid_odd), (far, far_odd)
        self.ssem, self.rsem, self.fsem = ssem, rsem, fsem

    def copy(self, src, dst, a, step, which, target):
        return pltpu.make_async_remote_copy(
            src_ref=src, dst_ref=dst, send_sem=self.ssem.at[a, step, which], recv_sem=self.rsem.at[a, step, which],
            device_id=target, device_id_type=MESH)

    def core_copies(self, a):
        return [self.copy(self.out[w].at[a], self.first[w].at[a], a, 0, w, self.where["mate"]) for w in (0, 1)]

    def axis_copies(self, a):
        copies = []
        for step in (1, 2, 3):
            to = list(self.at)
            to[a] = lax.rem(to[a] + step, 4)
            block = pl.ds(to[a] * 16, 16)
            copies += [self.copy(self.acc[w].at[a, block], self.near[w].at[a, step - 1], a, step, w,
                                 place(device(*to, self.core))) for w in (0, 1)]
        return copies

    def plane(self, a):
        return self.at[(a + 1) % 3] * 4 + self.at[(a + 2) % 3]

    def plane_copies(self, a, o, k):
        to = list(self.at)
        to[(a + 1) % 3], to[(a + 2) % 3] = o // 4, lax.rem(o, 4)
        slot = self.core * 16 + self.plane(a)
        return [pltpu.make_async_remote_copy(
            src_ref=src, dst_ref=self.far[w].at[a, slot], send_sem=self.fsem.at[0, a, w], recv_sem=self.fsem.at[1, a, w],
            device_id=place(device(*to, k)), device_id_type=MESH)
            for w, src in ((0, self.mid[0].at[a, o, k]), (1, self.mid[1].at[a, o]))]

    def plane_whole(self, a, w):
        part = self.far[w].at[a, pl.ds(0, 31)]
        return pltpu.make_async_remote_copy(
            src_ref=part, dst_ref=part, send_sem=self.fsem.at[0, a, w], recv_sem=self.fsem.at[1, a, w],
            device_id=self.where["mate"], device_id_type=MESH)

    @staticmethod
    def put(value, main, odd, a):
        rows = value[0:1024].reshape(64, 16, LANES).astype(BF)
        rest = value[1024:1152].reshape(64, 2, LANES).astype(BF)
        for b in range(64):
            main[a, turned(b, a)] = rows[b]
            odd[a, turned(b, a)] = rest[b]

    def start(self, product):
        for mine in (0, 1):
            @pl.when(self.core == mine)
            def _():
                for a in (2, 1, 0):
                    self.put(product(3 * (1 - mine) + a), *self.out, a)
                    for c in self.core_copies(a):
                        c.start()
                for a in (2, 1, 0):
                    self.put(product(3 * mine + a), *self.acc, a)

    def begin(self):
        for a in (2, 1, 0):
            for c in self.core_copies(a):
                c.wait_recv()
            for w in (0, 1):
                self.acc[w][a] = self.acc[w][a] + self.first[w][a]
            for c in self.axis_copies(a):
                c.start()

    def spread(self):
        for a in (2, 1, 0):
            for c in self.axis_copies(a):
                c.wait_recv()
            mine = pl.ds(self.at[a] * 16, 16)
            total, rest = (self.acc[w][a, mine].astype(F32) + self.near[w][a, 0].astype(F32)
                           + self.near[w][a, 1].astype(F32) + self.near[w][a, 2].astype(F32) for w in (0, 1))
            self.mid[0][a] = total.reshape(16, 2, 8, LANES).astype(BF)
            self.mid[1][a] = rest.astype(BF)
            here = self.plane(a)
            for c in self.plane_copies(a, here, 1 - self.core):
                c.start()

            @pl.loop(0, 5)
            def _(i):
                for u in range(3):
                    o = lax.rem(here + 1 + i * 3 + u, 16)
                    for k in (0, 1):
                        for c in self.plane_copies(a, o, k):
                            c.start()

    def finish(self, out_qkv, out_out):
        for a in (2, 1, 0):
            for w in (0, 1):
                self.plane_whole(a, w).wait_recv()
            here = self.plane(a)
            self.far[0][a, self.core * 16 + here] = self.mid[0][a, here, self.core]
            self.far[1][a, self.core * 16 + here] = self.mid[1][a, here]
            for half in (0, 1):
                chunk = 3 * half + a
                blocks = pl.ds(half * 16, 16)
                total = jnp.sum(self.far[0][a, blocks].astype(F32), axis=0)
                both = jnp.sum(self.far[1][a, blocks].astype(F32), axis=0)
                for rows, value in ((pl.ds(0, 8), total), (pl.ds(8, 1), jnp.where(self.core == 0, both[0:1], both[1:2]))):
                    if chunk < 4:
                        out_qkv[rows, chunk * LANES:(chunk + 1) * LANES] = value
                    elif chunk == 4:
                        out_qkv[rows, 1536:1728] = value[:, 0:192]
                        out_out[rows, 0:192] = value[:, 192:384]
                    else:
                        out_out[rows, 192:576] = value

    def drain(self):
        for a in range(3):
            for c in self.core_copies(a) + self.axis_copies(a):
                c.wait_send()
            for w in (0, 1):
                self.plane_whole(a, w).wait_send()


def kernel(tokens, cotangent, w_qkv_space, w_out_space, w_qkv_time, w_out_time,
           grad_tokens, gq_space, go_space, gq_time, go_time,
           tok, cot, wqs, wos, wqt, wot,
           snd_c, rcv_c, snd_m, rcv_m, snd_r, rcv_r,
           qkv_s, qkv_t, ga_ref, act, attp_t, attp_s, h_t, g_t, h_s, perm, weave, out_m, out_o, *rest):
    time_refs, space_refs = rest[0:10], rest[10:20]
    load_sem, local_sem, a2a_send, a2a_recv = rest[20:24]
    time_sems, space_sems = rest[24:27], rest[27:30]
    node, chip = lax.axis_index("node"), lax.axis_index("chip")
    me = node * 8 + chip
    barrier = pltpu.get_barrier_semaphore()

    def others(body):
        @pl.loop(0, 18)
        def _(i):
            for u in range(7):
                body(lax.rem(me + 1 + i * 7 + u, N))
        body(lax.rem(me + 127, N))

    others(lambda d: pl.semaphore_signal(barrier, inc=1, device_id=place(d), device_id_type=MESH))

    loads = [pltpu.make_async_copy(src, dst, load_sem.at[i]) for i, (src, dst) in enumerate(
        ((cotangent, cot), (tokens, tok), (w_qkv_space, wqs), (w_out_space, wos), (w_qkv_time, wqt), (w_out_time, wot)))]
    for c in loads:
        c.start()

    core = lax.rem(node, 2)
    x, y, z = chip // 2, lax.rem(node // 2, 4), lax.rem(chip, 2) * 2 + node // 8

    where = {"core": core, "at": (x, y, z), "mate": place(device(x, y, z, 1 - core))}

    to = lax.broadcasted_iota(jnp.int32, (S, S), 0)
    fro = lax.broadcasted_iota(jnp.int32, (S, S), 1)
    weave[...] = jnp.where((to % 2) * 128 + to // 2 == fro, 1.0, 0.0).astype(BF)

    def pieces(rows_of, c, dst):
        both = jnp.concatenate([rows_of[0, pl.ds(c * 128, 128)], rows_of[1, pl.ds(c * 128, 128)]], axis=0)
        dst[c] = mm(weave[...], both).astype(BF).reshape(128, 2, D)

    def exchange(kind, c, src, dst):
        pltpu.make_async_copy(src.at[c, me], dst.at[c, me], local_sem.at[kind, c]).start()
        others(lambda d: pltpu.make_async_remote_copy(
            src_ref=src.at[c, d], dst_ref=dst.at[c, me], send_sem=a2a_send.at[kind, c], recv_sem=a2a_recv.at[kind, c],
            device_id=place(d), device_id_type=MESH).start())

    def whole(kind, c, src, dst):
        return pltpu.make_async_remote_copy(
            src_ref=src.at[c, pl.ds(0, N - 1)], dst_ref=dst.at[c, pl.ds(0, N - 1)], send_sem=a2a_send.at[kind, c],
            recv_sem=a2a_recv.at[kind, c], device_id=where["mate"], device_id_type=MESH)

    def arrived(kind, c, src, dst):
        whole(kind, c, src, dst).wait_recv()
        pltpu.make_async_copy(src.at[c, me], dst.at[c, me], local_sem.at[kind, c]).wait()

    with jax.named_scope("load_cotangent"):
        loads[0].wait()
    for c in (0, 1):
        pieces(cot, c, snd_c)

    with jax.named_scope("load_space"):
        loads[1].wait()
        loads[2].wait()
        loads[3].wait()

    for f in (0, 1):
        lanes = pl.ds(f * S, S)
        with jax.named_scope("space_qkv"):
            qkv_s[f] = mm_nt(wqs[...], tok[f]).astype(BF)
        with jax.named_scope("space_heads"):
            heads(qkv_s.at[f], None, None, attp_s, lanes)
        with jax.named_scope("space_out"):
            cot[f] = (tok[f].astype(F32) + mm_tn(attp_s[192:768, lanes], wos[...])).astype(BF)
        if f == 0:
            with jax.named_scope("barrier"):
                pl.semaphore_wait(barrier, N - 1)
            exchange(0, 0, snd_c, rcv_c)

    pieces(cot, 0, snd_m)
    exchange(1, 0, snd_m, rcv_m)
    exchange(0, 1, snd_c, rcv_c)
    pieces(cot, 1, snd_m)
    exchange(1, 1, snd_m, rcv_m)

    def sources(code, pair, row):
        gx, gy, gz = code // 16, (code // 4) % 4, code % 4
        return 9 * ((gz % 2) * 64 + gy * 16 + pair * 8 + gx * 2 + gz // 2) + row

    at = lax.broadcasted_iota(jnp.int32, (1024, 1), 0)
    perm[0:1024, :] = jnp.where(
        sources(at // 16, (at // 8) % 2, at % 8) == lax.broadcasted_iota(jnp.int32, (1024, D), 1), 1.0, 0.0).astype(BF)
    at = lax.broadcasted_iota(jnp.int32, (128, 1), 0)
    perm[1024:D, :] = jnp.where(
        sources(at // 2, at % 2, 8) == lax.broadcasted_iota(jnp.int32, (128, D), 1), 1.0, 0.0).astype(BF)
    for ref, row in ((act, 1728), (attp_t, 0), (attp_s, 0)):
        ref[row:row + 192, :] = jnp.zeros((192, 512), BF)
    for f in (0, 1):
        h_s[:, f * S:(f + 1) * S] = mm_nt(perm[...], tok[f]).astype(BF)

    sides = [jnp.concatenate([attp_s[:, c * 128:(c + 1) * 128], attp_s[:, S + c * 128:S + (c + 1) * 128]], axis=1) for c in (0, 1)]
    for c in (0, 1):
        attp_s[:, c * S:(c + 1) * S] = mm_nt(sides[c], weave[...]).astype(BF)

    loads[4].wait()
    loads[5].wait()

    @pl.loop(0, 2)
    def _(c):
        lanes = pl.ds(pl.multiple_of(c * S, S), S)
        with jax.named_scope("wait_cotangent"):
            arrived(0, c, snd_c, rcv_c)
        ga_ref[...] = mm_nt(wot[...], rcv_c[c].reshape(S, D)).astype(BF)
        with jax.named_scope("wait_hidden"):
            arrived(1, c, snd_m, rcv_m)
        with jax.named_scope("time_qkv"):
            qkv_t[...] = mm_nt(wqt[...], rcv_m[c].reshape(S, D)).astype(BF)
        with jax.named_scope("time_heads"):
            heads(qkv_t, ga_ref, act, attp_t, lanes)
        with jax.named_scope("time_back"):
            up = rcv_c[c].reshape(S, D)
            back = (up.astype(F32) + mm_tn(act[0:1728, lanes], wqt[...])).astype(BF)
            snd_r[c] = back.reshape(128, 2, D)
        with jax.named_scope("time_send"):
            exchange(2, c, snd_r, rcv_r)

    for c in (0, 1):
        h_t[:, c * S:(c + 1) * S] = mm_nt(perm[...], rcv_m[c].reshape(S, D)).astype(BF)
        g_t[:, c * S:(c + 1) * S] = mm_nt(perm[...], rcv_c[c].reshape(S, D)).astype(BF)

    def product_of(h_t, attp):
        def product(chunk):
            rows = pl.ds(chunk * LANES, LANES)
            if chunk < 4:
                return mm_nt(h_t[...], act[rows, :])
            right = mm_nt(g_t[...], attp[pl.ds((chunk - 4) * LANES, LANES), :])
            return right + mm_nt(h_t[...], act[rows, :]) if chunk == 4 else right
        return product

    def summed(i, refs, sems):
        return Reduce(where, *refs[0:2], out_m.at[i], out_o.at[i], *refs[2:], *sems)

    time, space = summed(0, time_refs, time_sems), summed(1, space_refs, space_sems)
    with jax.named_scope("time_products"):
        time.start(product_of(h_t, attp_t))
    with jax.named_scope("time_begin"):
        time.begin()

    for c in (0, 1):
        with jax.named_scope("wait_back"):
            arrived(2, c, snd_r, rcv_r)
        g_t[:, c * S:(c + 1) * S] = mm_nt(perm[...], rcv_r[c].reshape(S, D)).astype(BF)
        both = mm_tn(weave[...], rcv_r[c].reshape(S, D)).astype(BF)
        cot[0, pl.ds(c * 128, 128)] = both[0:128]
        cot[1, pl.ds(c * 128, 128)] = both[128:256]

    for f in (0, 1):
        lanes = pl.ds(f * S, S)
        with jax.named_scope("space_ga"):
            ga_ref[...] = mm_nt(wos[...], cot[f]).astype(BF)
        with jax.named_scope("space_heads_back"):
            heads(qkv_s.at[f], ga_ref, act, None, lanes)
    with jax.named_scope("space_products"):
        space.start(product_of(h_s, attp_s))
    with jax.named_scope("space_begin"):
        space.begin()
    with jax.named_scope("time_spread"):
        time.spread()
    for f in (0, 1):
        with jax.named_scope("space_back"):
            grad_tokens[f] = (cot[f].astype(F32) + mm_tn(act[0:1728, pl.ds(f * S, S)], wqs[...])).astype(BF)
    with jax.named_scope("time_finish"):
        time.finish(gq_time, go_time)
    with jax.named_scope("space_spread"):
        space.spread()
    with jax.named_scope("space_finish"):
        space.finish(gq_space, go_space)

    for kind, (src, dst) in enumerate(((snd_c, rcv_c), (snd_m, rcv_m), (snd_r, rcv_r))):
        for c in (0, 1):
            whole(kind, c, src, dst).wait_send()
    time.drain()
    space.drain()


def hand_over(*refs):
    copies = [pltpu.make_async_copy(refs[i], refs[5 + i], refs[10].at[i]) for i in range(5)]
    for c in copies:
        c.start()
    for c in copies:
        c.wait()


def body(tokens, cotangent, w_qkv_space, w_out_space, w_qkv_time, w_out_time):
    vm = pltpu.VMEM
    pieces = vm((2, N, 2, D), BF)

    def main(n):
        return vm((3, n, 16, LANES), BF)

    def odd(n):
        return vm((3, n, 2, LANES), BF)

    dma = pltpu.SemaphoreType.DMA
    halves = [main(64), odd(64), main(64), odd(64), vm((3, 3, 16, 16, LANES), BF), vm((3, 3, 16, 2, LANES), BF),
              vm((3, 16, 2, 8, LANES), BF), odd(16), vm((3, 32, 8, LANES), BF), odd(32)]
    sums = [dma((3, 4, 2)), dma((3, 4, 2)), dma((2, 3, 2))]
    hbm, inside = pl.BlockSpec(memory_space=pl.ANY), pl.BlockSpec(memory_space=pltpu.VMEM)
    found = pl.pallas_call(
        kernel,
        out_shape=(
            jax.ShapeDtypeStruct((2, S, D), BF),
            jax.ShapeDtypeStruct((9, 1728), F32),
            jax.ShapeDtypeStruct((9, INNER), F32),
            jax.ShapeDtypeStruct((9, 1728), F32),
            jax.ShapeDtypeStruct((9, INNER), F32),
        ),
        in_specs=[hbm] * 6,
        out_specs=(inside,) * 5,
        scratch_shapes=[
            vm((2, S, D), BF), vm((2, S, D), BF), vm((1728, D), BF), vm((INNER, D), BF), vm((1728, D), BF), vm((INNER, D), BF),
            *[pieces] * 6,
            vm((2, 1728, S), BF), vm((1728, S), BF), vm((INNER, S), BF), vm((1920, 512), BF), vm((768, 512), BF), vm((768, 512), BF),
            vm((D, 512), BF), vm((D, 512), BF), vm((D, 512), BF), vm((D, D), BF), vm((S, S), BF),
            vm((2, 3, 64, 16, LANES), BF), vm((2, 3, 64, 2, LANES), BF),
            *halves, *halves,
            dma((6,)), dma((3, 2)), dma((3, 2)), dma((3, 2)), *sums, *sums,
        ],
        compiler_params=pltpu.CompilerParams(
            collective_id=0, has_side_effects=True, vmem_limit_bytes=63 * 2**20),
    )(tokens, cotangent, w_qkv_space.T, w_out_space, w_qkv_time.T, w_out_time)
    grad_tokens, gq_space, go_space, gq_time, go_time = pl.pallas_call(
        hand_over,
        out_shape=tuple(jax.ShapeDtypeStruct(a.shape, a.dtype) for a in found),
        in_specs=[hbm] * 5,
        out_specs=(inside,) * 5,
        scratch_shapes=[dma((5,))],
        compiler_params=pltpu.CompilerParams(vmem_limit_bytes=63 * 2**20),
    )(*found)
    return grad_tokens, gq_space, go_space.T, gq_time, go_time.T


def solution(mesh):
    rows = P(("node", "chip"), None, None)
    return jax.shard_map(
        body,
        mesh=mesh,
        in_specs=(rows, rows, P(), P(), P(), P()),
        out_specs=(rows, P(("node", "chip"), None), P(None, ("node", "chip")),
                   P(("node", "chip"), None), P(None, ("node", "chip"))),
        check_vma=False,
    )
```
